256 devices in a mesh: dp: 4 (over z_lo), seq: 32 (over x, y, core), tp: 2 (over z_hi).
Axes of the slice: x: 4, y: 4, z: 8 (z_hi: 2, z_lo: 4; z = z_hi * 4 + z_lo), core: 2. Of those that a mesh axis runs over, the one named last changes fastest.
Arguments:
- query: bfloat16 [4, 16384, 512], P('dp', 'seq', 'tp'), may hold values from -6 to 6
- key_in: bfloat16 [4, 16384, 512], P('dp', 'seq', 'tp'), may hold values from -6 to 6
- value: bfloat16 [4, 16384, 512], P('dp', 'seq', 'tp'), may hold values from -6 to 6
- grad_out: bfloat16 [4, 16384, 512], P('dp', 'seq', 'tp'), may hold values from -6 to 6
- filter_taps: float32 [16384, 512], P('seq', 'tp'), may hold values from -1 to 1, as said below
Outputs:
- grad_query: bfloat16 [4, 16384, 512], P('dp', 'seq', 'tp')
- grad_key: bfloat16 [4, 16384, 512], P('dp', 'seq', 'tp')
- grad_value: bfloat16 [4, 16384, 512], P('dp', 'seq', 'tp')
- filter_grad: float32 [16384, 512], P('seq', 'tp')
The draws below stay inside these ranges and needn't reach their ends.
Inputs may be any that keep to these rules, and one draw needn't show every extreme that they name: `filter_taps`: filter taps of each channel over 16384 positions.
All inputs are finite; a program needn't handle non-finite values.
Results may differ from the reference program's by a relative error of at most 0.0015.
Values sent between devices are 32-bit elements; how exact they have to be, the bound alone decides.
A program may use at most 128 MiB of HBM per device.

```python
import math
import jax
import jax.numpy as jnp

GROUP_CHANNELS = 512
WINDOW_LENGTH = 16384
WINDOWS = 4


def draw_filter_taps(key, part):
    key = jax.random.fold_in(key, 7)
    random_keys = jax.random.split(key, 8)
    slow_share = 0.5
    random_jitter = jax.random.truncated_normal(random_keys[0], -3.0, 3.0, (WINDOW_LENGTH, GROUP_CHANNELS), jnp.float32)
    tail_jitter = jax.random.truncated_normal(random_keys[6], -3.0, 3.0, (WINDOW_LENGTH, GROUP_CHANNELS), jnp.float32)
    slow_mask = jax.random.bernoulli(random_keys[1], slow_share, (GROUP_CHANNELS,))
    slow_rate = jax.random.uniform(random_keys[2], (GROUP_CHANNELS,), jnp.float32, 0.1, 2.0) / WINDOW_LENGTH
    fast_rate = jax.random.uniform(random_keys[3], (GROUP_CHANNELS,), jnp.float32, 1.0 / 50.0, 1.0 / 30.0)
    rates = jnp.where(slow_mask, slow_rate, fast_rate)
    time_points = jnp.arange(WINDOW_LENGTH, dtype=jnp.float32)[:, None]
    decay_profile = jnp.exp(-time_points * rates[None, :])
    spike_location = jax.random.randint(random_keys[4], (4,), 0, WINDOW_LENGTH).astype(jnp.float32)
    spike_factor = jax.random.uniform(random_keys[5], (4, GROUP_CHANNELS), jnp.float32, 0.5, 0.8)
    log_spike = jnp.zeros((WINDOW_LENGTH, GROUP_CHANNELS), jnp.float32)
    for spike_pulse in range(4):
        kept_flags = (time_points >= spike_location[spike_pulse]).astype(jnp.float32)
        log_spike = log_spike + kept_flags * jnp.log(spike_factor[spike_pulse])[None, :]
    peak_height = jnp.sqrt(2.0 * rates + 1.0 / WINDOW_LENGTH)[None, :]
    tail_rate = jax.random.uniform(random_keys[7], (GROUP_CHANNELS,), jnp.float32, 0.1, 2.0) / WINDOW_LENGTH
    tail_height = 0.15 * jnp.sqrt(2.0 * tail_rate + 1.0 / WINDOW_LENGTH)[None, :]
    tail_part = tail_jitter * jnp.exp(-time_points * tail_rate[None, :]) * tail_height
    return (random_jitter * decay_profile * peak_height + tail_part) * jnp.exp(log_spike)


def block_scale(key, extent, cuts, least, top_value):
    def one(dim, blocks):
        draws = jax.random.uniform(jax.random.fold_in(jax.random.fold_in(key, 6), dim), (blocks,), jnp.float32, least / len(cuts), top_value / len(cuts))
        return jnp.repeat(jnp.exp(draws), extent[dim] // blocks).reshape((-1,) + (1,) * (len(extent) - dim - 1))

    level = one(*cuts[0])
    for cut in cuts[1:]:
        level = level * one(*cut)
    return level


def noise(key, extent, spread, reach, pieces=(), kind=jnp.bfloat16):
    entries = jax.random.normal(key, extent, jnp.float32) * spread
    if len(pieces) > 0:
        entries = block_scale(key, extent, pieces, -0.22, 0.18) * entries
    return jnp.clip(entries, min=-reach, max=reach).astype(kind)


def setup_inputs(seed: int = 0) -> dict:
    key_list = jax.random.split(jax.random.key(seed), 6)
    return {
        "query": noise(key_list[0], (WINDOWS, WINDOW_LENGTH, GROUP_CHANNELS), 1.0, 6.0, ((0, 4), (1, 32), (2, 2))),
        "key_in": noise(key_list[1], (WINDOWS, WINDOW_LENGTH, GROUP_CHANNELS), 1.0, 6.0, ((0, 4), (1, 32), (2, 2))),
        "value": noise(key_list[2], (WINDOWS, WINDOW_LENGTH, GROUP_CHANNELS), 1.0, 6.0, ((0, 4), (1, 32), (2, 2))),
        "grad_out": noise(key_list[3], (WINDOWS, WINDOW_LENGTH, GROUP_CHANNELS), 1.0, 6.0, ((0, 4), (1, 32), (2, 2))),
        "filter_taps": draw_filter_taps(jax.random.fold_in(key_list[5], 71), 0),
    }


def reference(query, key_in, value, grad_out, filter_taps):
    total_len = 2 * WINDOW_LENGTH
    taps_spec = jnp.fft.fft(filter_taps, n=total_len, axis=0)
    grads_query = []
    grads_key = []
    grads_value = []
    corr_sum = None
    for window in range(WINDOWS):
        query_f = query[window].astype(jnp.float32)
        key_f = key_in[window].astype(jnp.float32)
        value_f = value[window].astype(jnp.float32)
        grad_f = grad_out[window].astype(jnp.float32)
        gated = key_f * value_f
        dgate = grad_f * query_f
        gate_spec = jnp.fft.fft(gated, n=total_len, axis=0)
        dgate_spec = jnp.fft.fft(dgate, n=total_len, axis=0)
        convolved = jnp.real(jnp.fft.ifft(taps_spec * gate_spec, axis=0))[:WINDOW_LENGTH]
        adjoint = jnp.real(jnp.fft.ifft(jnp.conj(taps_spec) * dgate_spec, axis=0))[:WINDOW_LENGTH]
        correlation = jnp.conj(gate_spec) * dgate_spec
        corr_sum = correlation if window == 0 else corr_sum + correlation
        grads_query.append((grad_f * convolved).astype(jnp.bfloat16))
        grads_key.append((adjoint * value_f).astype(jnp.bfloat16))
        grads_value.append((adjoint * key_f).astype(jnp.bfloat16))
    filter_grad = jnp.real(jnp.fft.ifft(corr_sum, axis=0))[:WINDOW_LENGTH] * (1.0 / math.sqrt(WINDOWS * WINDOW_LENGTH))
    return (jnp.stack(grads_query), jnp.stack(grads_key), jnp.stack(grads_value), filter_grad)
```

```python
import functools
import math

import jax
import jax.numpy as jnp
import ml_dtypes
import numpy as np
from jax import lax
from jax.experimental import pallas as pl
from jax.experimental.pallas import tpu as pltpu
from jax.sharding import PartitionSpec as P

MESH = pl.DeviceIdType.MESH
SEQ = 32
DP = 4
LANES = 128
ROWS = 1024
POINTS = 16384
BF = jnp.bfloat16
F32 = jnp.float32


def halves(table):
    table = np.asarray(table, np.float32)
    high = table.astype(ml_dtypes.bfloat16)
    low = (table - high.astype(np.float32)).astype(ml_dtypes.bfloat16)
    return high, low


def make_tables():
    idx = np.arange(LANES, dtype=np.float64)
    turn = 2.0 * math.pi * np.outer(idx + 0.25, idx) / LANES
    first = np.concatenate([np.cos(turn), -np.sin(turn)], axis=0)
    twist = 2.0 * math.pi * np.outer(idx + 0.25, idx) / POINTS
    plain = 2.0 * math.pi * np.outer(idx, idx) / LANES
    cos, sin = np.cos(plain), np.sin(plain)
    second = np.block([[cos, -sin], [sin, cos]])
    back = np.block([[cos, sin], [-sin, cos]])
    last = np.concatenate([np.cos(turn).T, -np.sin(turn).T], axis=1) / POINTS
    first_h, first_l = halves(first)
    first_cat = np.concatenate([first_h, first_h], axis=1)
    second_h, second_l = halves(second)
    back_h, back_l = halves(back)
    last_h, last_l = halves(last)
    return (
        first_cat,
        first_l,
        second_h,
        second_l,
        back_h,
        back_l,
        last_h,
        last_l,
        np.cos(twist).astype(np.float32),
        (-np.sin(twist)).astype(np.float32),
    )


def split(x):
    high = x.astype(BF)
    return high, (x - high.astype(F32)).astype(BF)


def dot(a, b):
    return jnp.dot(a, b, preferred_element_type=F32)


def kernel(
    query, key_in, value, grad, taps,
    first_cat, first_l, second_h, second_l, back_h, back_l, last_h, last_l, turn_re, turn_im,
    out_query, out_key, out_value, out_filter,
    s_gate, s_dgate, s_taps, s_corr, s_conv, s_adj,
    r_gate, r_dgate, r_taps, r_corr, r_conv, r_adj,
    f_gate, f_dgate, f_taps,
    z_part, z_sum, z_full,
    send_sem, recv_sem, z_send, z_recv,
):
    dp = lax.axis_index("dp")
    me = lax.axis_index("seq")
    tp = lax.axis_index("tp")
    chip, core = me // 2, lax.rem(me, 2)
    x_at, y_at = chip // 4, lax.rem(chip, 4)

    def partner(step):
        dc = lax.rem(step, 2)
        dy = lax.rem(step // 2, 4)
        dx = step // 8
        return (lax.rem(x_at + dx, 4) * 4 + lax.rem(y_at + dy, 4)) * 2 + lax.rem(core + dc, 2)

    barrier = pltpu.get_barrier_semaphore()

    @pl.loop(1, SEQ)
    def _(step):
        pl.semaphore_signal(barrier, inc=1, device_id=(dp, partner(step), tp), device_id_type=MESH)

    for step in range(1, DP):
        pl.semaphore_signal(
            barrier, inc=1, device_id=(lax.rem(dp + step, DP), me, tp), device_id_type=MESH
        )

    def pack(out, block):
        for a in range(4):
            for h in range(2):
                tile = block(pl.ds(LANES * a, LANES), pl.ds(LANES * h, LANES)).T
                for d in range(16):
                    out[pl.ds((16 * h + d) * 32 + 8 * a, 8), :] = tile[8 * d : 8 * d + 8, :]

    def unpack(ref, a, h):
        return jnp.concatenate(
            [ref[pl.ds((16 * h + d) * 32 + 8 * a, 8), :] for d in range(16)], axis=0
        ).T

    def exchange(index, src, dst):
        @pl.loop(1, SEQ)
        def _(step):
            to = partner(step)
            pltpu.make_async_remote_copy(
                src_ref=src.at[pl.ds(pl.multiple_of(to * 32, 32), 32)],
                dst_ref=dst.at[pl.ds(pl.multiple_of(me * 32, 32), 32)],
                send_sem=send_sem.at[index],
                recv_sem=recv_sem.at[index],
                device_id=(dp, to, tp),
                device_id_type=MESH,
            ).start()

        mine = pl.ds(pl.multiple_of(me * 32, 32), 32)
        pltpu.make_async_copy(src.at[mine], dst.at[mine], recv_sem.at[index]).start()

    def arrived(index, dst):
        pltpu.make_async_copy(dst, dst, recv_sem.at[index]).wait()

    def sent(index, src):
        part = src.at[pl.ds(0, ROWS - 32)]
        pltpu.make_async_copy(part, part, send_sem.at[index]).wait()

    def forward(src, spec):
        @pl.loop(0, 4)
        def _(pair):
            y = jnp.concatenate(
                [src[pl.ds(2 * pair + j, LANES, stride=8), :] for j in range(2)], axis=1
            )
            yh, yl = split(y)
            a = dot(first_cat[...], jnp.concatenate([yh, yl], axis=0)) + dot(first_l[...], yh)
            rows = []
            for j in range(2):
                re, im = a[:LANES, LANES * j : LANES * (j + 1)], a[LANES:, LANES * j : LANES * (j + 1)]
                wr, wi = turn_re[...], turn_im[...]
                rows.append(jnp.concatenate([re * wr - im * wi, re * wi + im * wr], axis=1))
            ph, pw = split(jnp.concatenate(rows, axis=0))
            spec[pl.ds(pl.multiple_of(pair * 256, 256), 256), :] = (
                dot(ph, second_h[...]) + dot(pw, second_h[...]) + dot(ph, second_l[...])
            )

    def inverse(left, right, conj, dst):
        @pl.loop(0, 4)
        def _(pair):
            at = pl.ds(pl.multiple_of(pair * 256, 256), 256)
            lr, li = left[at, :LANES], left[at, LANES:]
            rr, ri = right[at, :LANES], right[at, LANES:]
            if conj:
                prod = [lr * rr + li * ri, lr * ri - li * rr]
            else:
                prod = [lr * rr - li * ri, lr * ri + li * rr]
            ph, pw = split(jnp.concatenate(prod, axis=1))
            b = dot(ph, back_h[...]) + dot(pw, back_h[...]) + dot(ph, back_l[...])
            cols = []
            for j in range(2):
                re, im = b[LANES * j : LANES * (j + 1), :LANES], b[LANES * j : LANES * (j + 1), LANES:]
                wr, wi = turn_re[...], turn_im[...]
                cols.append(jnp.concatenate([re * wr + im * wi, im * wr - re * wi], axis=0))
            zh, zl = split(jnp.concatenate(cols, axis=1))
            y = dot(last_h[...], zh) + dot(last_h[...], zl) + dot(last_l[...], zh)
            for j in range(2):
                dst[pl.ds(2 * pair + j, LANES, stride=8), :] = y[:, LANES * j : LANES * (j + 1)]

    pack(s_gate, lambda p, c: key_in[0, p, c].astype(F32) * value[0, p, c].astype(F32))
    pl.semaphore_wait(barrier, SEQ + DP - 2)
    exchange(0, s_gate, r_gate)
    pack(s_dgate, lambda p, c: grad[0, p, c].astype(F32) * query[0, p, c].astype(F32))
    exchange(1, s_dgate, r_dgate)
    pack(s_taps, lambda p, c: taps[p, c])
    exchange(2, s_taps, r_taps)

    arrived(0, r_gate)
    forward(r_gate, f_gate)
    arrived(1, r_dgate)
    forward(r_dgate, f_dgate)
    inverse(f_gate, f_dgate, True, s_corr)
    exchange(3, s_corr, r_corr)
    arrived(2, r_taps)
    forward(r_taps, f_taps)
    inverse(f_taps, f_gate, False, s_conv)
    exchange(4, s_conv, r_conv)
    inverse(f_taps, f_dgate, True, s_adj)
    exchange(5, s_adj, r_adj)

    arrived(3, r_corr)
    for step in range(1, DP):
        to = lax.rem(dp + step, DP)
        pltpu.make_async_remote_copy(
            src_ref=r_corr.at[pl.ds(pl.multiple_of(to * 256, 256), 256)],
            dst_ref=z_part.at[step - 1],
            send_sem=z_send.at[0],
            recv_sem=z_recv.at[0],
            device_id=(to, me, tp),
            device_id_type=MESH,
        ).start()
    pltpu.make_async_copy(z_part, z_part, z_recv.at[0]).wait()
    own = pl.ds(pl.multiple_of(dp * 256, 256), 256)
    z_sum[...] = (r_corr[own, :] + z_part[0] + z_part[1] + z_part[2]) * (
        1.0 / math.sqrt(DP * POINTS)
    )
    for step in range(1, DP):
        pltpu.make_async_remote_copy(
            src_ref=z_sum,
            dst_ref=z_full.at[own],
            send_sem=z_send.at[1],
            recv_sem=z_recv.at[1],
            device_id=(lax.rem(dp + step, DP), me, tp),
            device_id_type=MESH,
        ).start()
    pltpu.make_async_copy(z_sum, z_full.at[own], z_recv.at[1]).start()

    arrived(4, r_conv)
    for a in range(4):
        for h in range(2):
            p, c = pl.ds(LANES * a, LANES), pl.ds(LANES * h, LANES)
            out_query[0, p, c] = (grad[0, p, c].astype(F32) * unpack(r_conv, a, h)).astype(BF)
    arrived(5, r_adj)
    for a in range(4):
        for h in range(2):
            p, c = pl.ds(LANES * a, LANES), pl.ds(LANES * h, LANES)
            adjoint = unpack(r_adj, a, h)
            out_key[0, p, c] = (adjoint * value[0, p, c].astype(F32)).astype(BF)
            out_value[0, p, c] = (adjoint * key_in[0, p, c].astype(F32)).astype(BF)
    pltpu.make_async_copy(z_full, z_full, z_recv.at[1]).wait()
    for a in range(4):
        for h in range(2):
            out_filter[pl.ds(LANES * a, LANES), pl.ds(LANES * h, LANES)] = unpack(z_full, a, h)

    for index, src in enumerate((s_gate, s_dgate, s_taps, s_corr, s_conv, s_adj)):
        sent(index, src)
    for index in range(2):
        pltpu.make_async_copy(z_part, z_part, z_send.at[index]).wait()


def shards(query, key_in, value, grad_out, filter_taps):
    vmem = pl.BlockSpec(memory_space=pltpu.VMEM)
    tables = tuple(jnp.asarray(t) for t in make_tables())
    block = pltpu.VMEM((ROWS, LANES), F32)
    return pl.pallas_call(
        kernel,
        out_shape=(
            jax.ShapeDtypeStruct(query.shape, BF),
            jax.ShapeDtypeStruct(query.shape, BF),
            jax.ShapeDtypeStruct(query.shape, BF),
            jax.ShapeDtypeStruct(filter_taps.shape, F32),
        ),
        in_specs=[vmem] * (5 + len(tables)),
        out_specs=(vmem,) * 4,
        scratch_shapes=[block] * 12
        + [pltpu.VMEM((ROWS, 2 * LANES), F32)] * 3
        + [
            pltpu.VMEM((DP - 1, ROWS // DP, LANES), F32),
            pltpu.VMEM((ROWS // DP, LANES), F32),
            block,
            pltpu.SemaphoreType.DMA((6,)),
            pltpu.SemaphoreType.DMA((6,)),
            pltpu.SemaphoreType.DMA((2,)),
            pltpu.SemaphoreType.DMA((2,)),
        ],
        compiler_params=pltpu.CompilerParams(
            collective_id=0, has_side_effects=True, vmem_limit_bytes=48 * 1024 * 1024
        ),
    )(query, key_in, value, grad_out, filter_taps, *tables)


def solution(mesh):
    wide = P("dp", "seq", "tp")
    narrow = P("seq", "tp")
    return jax.shard_map(
        shards,
        mesh=mesh,
        in_specs=(wide, wide, wide, wide, narrow),
        out_specs=(wide, wide, wide, narrow),
        check_vma=False,
    )
```

```python
import functools
import math

import jax
import jax.numpy as jnp
import ml_dtypes
import numpy as np
from jax import lax
from jax.experimental import pallas as pl
from jax.experimental.pallas import tpu as pltpu
from jax.sharding import PartitionSpec as P

MESH = pl.DeviceIdType.MESH
SEQ = 32
DP = 4
LANES = 128
ROWS = 1024
POINTS = 16384
BF = jnp.bfloat16
F32 = jnp.float32


def halves(table):
    table = np.asarray(table, np.float32)
    high = table.astype(ml_dtypes.bfloat16)
    low = (table - high.astype(np.float32)).astype(ml_dtypes.bfloat16)
    return high, low


def make_tables():
    idx = np.arange(LANES, dtype=np.float64)
    turn = 2.0 * math.pi * np.outer(idx + 0.25, idx) / LANES
    first = np.concatenate([np.cos(turn), -np.sin(turn)], axis=0)
    twist = 2.0 * math.pi * np.outer(idx + 0.25, idx) / POINTS
    plain = 2.0 * math.pi * np.outer(idx, idx) / LANES
    cos, sin = np.cos(plain), np.sin(plain)
    second = np.block([[cos, -sin], [sin, cos]])
    back = np.block([[cos, sin], [-sin, cos]])
    last = np.concatenate([np.cos(turn).T, -np.sin(turn).T], axis=1) / POINTS
    first_h, first_l = halves(first)
    mats = [
        np.concatenate([first_h, first_h], axis=1),
        np.concatenate([first_l, np.zeros_like(first_l)], axis=1),
        *halves(second),
        *halves(back),
        *halves(last),
    ]
    turns = [np.cos(twist), -np.sin(twist)]
    return np.concatenate(mats, axis=0), np.concatenate(turns, axis=0).astype(np.float32)


def split(x):
    high = x.astype(BF)
    return high, (x - high.astype(F32)).astype(BF)


def dot(a, b):
    return jnp.dot(a, b, preferred_element_type=F32)


def kernel(
    query_in, key_hbm, value_in, grad_in, taps_in, mats_in, turns_in,
    out_query, out_key, out_value, out_filter,
    query, key_in, value, grad, taps, mats, turns,
    o_query, o_key, o_value, o_filter,
    t_gd, t_taps, t_corr, t_ret, t_filt,
    s_gd, r_gd, s_taps, r_taps, s_ret, r_ret,
    f_gd, f_taps, c_part, z_part, z_sum, z_all,
    x_send, x_recv, m_send, m_recv, rs_send, rs_recv, ag_send, ag_recv,
    pair_send, pair_recv, load_sem, store_sem,
):
    dp = lax.axis_index("dp")
    me = lax.axis_index("seq")
    tp = lax.axis_index("tp")
    chip, core = me // 2, lax.rem(me, 2)
    x_at, y_at = chip // 4, lax.rem(chip, 4)
    odd = lax.rem(dp, 2)
    mate = dp + 1 - 2 * odd

    loads = [
        pltpu.make_async_copy(src, dst, load_sem.at[i])
        for i, (src, dst) in enumerate(
            (
                (key_hbm, key_in),
                (value_in, value),
                (grad_in, grad),
                (query_in, query),
                (taps_in, taps),
                (mats_in, mats),
                (turns_in, turns),
            )
        )
    ]
    for load in loads:
        load.start()
    first_cat = mats.at[pl.ds(0, 256)]
    first_l = mats.at[pl.ds(256, 256), pl.ds(0, LANES)]
    second_h, second_l, back_h, back_l = (mats.at[pl.ds(512 + 256 * i, 256)] for i in range(4))
    last_h, last_l = (mats.at[pl.ds(1536 + LANES * i, LANES)] for i in range(2))
    turn_re, turn_im = (turns.at[pl.ds(LANES * i, LANES)] for i in range(2))

    def partner(step):
        dc = lax.rem(step, 2)
        dy = lax.rem(step // 2, 4)
        dx = step // 8
        return (lax.rem(x_at + dx, 4) * 4 + lax.rem(y_at + dy, 4)) * 2 + lax.rem(core + dc, 2)

    barrier = pltpu.get_barrier_semaphore()

    @pl.loop(1, SEQ)
    def _(step):
        pl.semaphore_signal(barrier, inc=1, device_id=(dp, partner(step), tp), device_id_type=MESH)

    for step in range(1, DP):
        pl.semaphore_signal(
            barrier, inc=1, device_id=(lax.rem(dp + step, DP), me, tp), device_id_type=MESH
        )


    def exchange(index, src, dst, base):
        mine = pl.ds(pl.multiple_of(base + me * 16, 16), 16)

        @pl.loop(1, SEQ)
        def _(step):
            to = partner(step)
            pltpu.make_async_remote_copy(
                src_ref=src.at[pl.ds(pl.multiple_of(base + to * 16, 16), 16)],
                dst_ref=dst.at[mine],
                send_sem=x_send.at[index],
                recv_sem=x_recv.at[index],
                device_id=(dp, to, tp),
                device_id_type=MESH,
            ).start()

        pltpu.make_async_copy(src.at[mine], dst.at[mine], x_recv.at[index]).start()

    def arrived(index, dst, base):
        part = dst.at[pl.ds(pl.multiple_of(base, 512), 512)]
        pltpu.make_async_copy(part, part, x_recv.at[index]).wait()


    def transpose_gd(h):
        c = pl.ds(LANES * h, LANES)
        for sig, (left, right) in enumerate(((key_in, value), (grad, query))):
            for a in range(4):
                p = pl.ds(LANES * a, LANES)
                at = ((h * 2 + sig) * 4 + a) * LANES
                t_gd[pl.ds(at, LANES), :] = (left[0, p, c].astype(F32) * right[0, p, c].astype(F32)).T

    def pack_gd(p):
        for sig in range(2):
            for a in range(4):
                at = (((p // 2) * 2 + sig) * 4 + a) * LANES + 64 * (p % 2)
                for c in range(2):
                    s_gd[pl.ds(p * 512 + a * 4 + sig * 2 + c, 32, stride=16), :] = t_gd[
                        pl.ds(at + c, 32, stride=2), :
                    ]

    def pack_taps():
        for h in range(2):
            for a in range(4):
                at = (h * 4 + a) * LANES
                t_taps[pl.ds(at, LANES), :] = taps[pl.ds(LANES * a, LANES), pl.ds(LANES * h, LANES)].T
        for h in range(2):
            for a in range(4):
                at = (h * 4 + a) * LANES
                for c in range(2):
                    s_taps[pl.ds(a * 4 + h * 2 + c, 32, stride=16), :] = t_taps[
                        pl.ds(at + 64 * odd + c, 32, stride=2), :
                    ]


    def forward(src, base):
        y = jnp.concatenate([src[pl.ds(base + j, LANES, stride=4), :] for j in range(2)], axis=1)
        yh, yl = split(y)
        a = dot(first_cat[...], jnp.concatenate([yh, yl], axis=0)) + dot(first_l[...], yh)
        wr, wi = turn_re[...], turn_im[...]
        rows = []
        for j in range(2):
            re, im = a[:LANES, LANES * j : LANES * (j + 1)], a[LANES:, LANES * j : LANES * (j + 1)]
            rows.append(jnp.concatenate([re * wr - im * wi, re * wi + im * wr], axis=1))
        ph, pw = split(jnp.concatenate(rows, axis=0))
        return dot(ph, second_h[...]) + dot(pw, second_h[...]) + dot(ph, second_l[...])

    def inverse(left, right, conj):
        lr, li, rr, ri = left[:, :LANES], left[:, LANES:], right[:, :LANES], right[:, LANES:]
        if conj:
            prod = [lr * rr + li * ri, lr * ri - li * rr]
        else:
            prod = [lr * rr - li * ri, lr * ri + li * rr]
        ph, pw = split(jnp.concatenate(prod, axis=1))
        b = dot(ph, back_h[...]) + dot(pw, back_h[...]) + dot(ph, back_l[...])
        wr, wi = turn_re[...], turn_im[...]
        cols = []
        for j in range(2):
            re, im = b[LANES * j : LANES * (j + 1), :LANES], b[LANES * j : LANES * (j + 1), LANES:]
            cols.append(jnp.concatenate([re * wr + im * wi, im * wr - re * wi], axis=0))
        zh, zl = split(jnp.concatenate(cols, axis=1))
        return dot(last_h[...], zh) + dot(last_h[...], zl) + dot(last_l[...], zh)

    def spec_at(p, sig):
        return pl.ds(pl.multiple_of((p * 2 + sig) * 256, 256), 256)

    def gate_chunk(p):
        gate = forward(r_gd, p * 512)
        dgate = forward(r_gd, p * 512 + 2)
        f_gd[spec_at(p, 0), :] = gate
        f_gd[spec_at(p, 1), :] = dgate
        y = inverse(gate, dgate, True)
        for c in range(2):
            at = (p * 2 + c) * LANES
            t_corr[pl.ds(at, LANES), :] = y[:, LANES * c : LANES * (c + 1)]
            for a in range(4):
                c_part[pl.ds(p * 256 + a * 64 + c, 32, stride=2), :] = t_corr[
                    pl.ds(at + a, 32, stride=4), :
                ]
        for step in range(1, DP):
            to = lax.rem(dp + step, DP)
            pltpu.make_async_remote_copy(
                src_ref=c_part.at[pl.ds(pl.multiple_of(p * 256 + to * 64, 64), 64)],
                dst_ref=z_part.at[pl.ds((p * 3 + step - 1) * 64, 64)],
                send_sem=rs_send.at[p],
                recv_sem=rs_recv.at[p],
                device_id=(to, me, tp),
                device_id_type=MESH,
            ).start()

    def sum_chunk(p):
        part = z_part.at[pl.ds(p * 192, 192)]
        pltpu.make_async_copy(part, part, rs_recv.at[p]).wait()
        scale = 1.0 / math.sqrt(DP * POINTS)
        for c in range(2):
            total = c_part[pl.ds(p * 256 + dp * 64 + c, 32, stride=2), :]
            for step in range(DP - 1):
                total = total + z_part[pl.ds((p * 3 + step) * 64 + c, 32, stride=2), :]
            z_sum[:, 2 * p + c, :] = total * scale
        two = pl.ds(2 * p, 2)

        @pl.loop(1, SEQ)
        def _(step):
            to = partner(step)
            pltpu.make_async_remote_copy(
                src_ref=z_sum.at[to, two],
                dst_ref=z_all.at[dp, me, two],
                send_sem=m_send.at[p],
                recv_sem=m_recv.at[p],
                device_id=(dp, to, tp),
                device_id_type=MESH,
            ).start()

        pltpu.make_async_copy(z_sum.at[me, two], z_all.at[dp, me, two], m_recv.at[p]).start()

    def spread_chunk(p):
        part = z_all.at[dp, :, pl.ds(2 * p, 2)]
        pltpu.make_async_copy(part, part, m_recv.at[p]).wait()
        for step in range(1, DP):
            pltpu.make_async_remote_copy(
                src_ref=part,
                dst_ref=part,
                send_sem=ag_send.at[p],
                recv_sem=ag_recv.at[p],
                device_id=(lax.rem(dp + step, DP), me, tp),
                device_id_type=MESH,
            ).start()

    def forward_taps(half):
        base = pl.multiple_of(half * 512, 512)
        for h in range(2):
            f_taps[pl.ds(pl.multiple_of((2 * h + half) * 256, 256), 256), :] = forward(
                r_taps, base + 2 * h
            )

    def return_chunk(p):
        filt = f_taps[pl.ds(pl.multiple_of(p * 256, 256), 256), :]
        conv = inverse(filt, f_gd[spec_at(p, 0), :], False)
        adj = inverse(filt, f_gd[spec_at(p, 1), :], True)
        for v in range(4):
            y = (conv, adj)[v // 2]
            s_ret[pl.ds(p * 512 + v, LANES, stride=4), :] = y[:, LANES * (v % 2) : LANES * (v % 2 + 1)]
        exchange(5 + p, s_ret, r_ret, p * 512)

    def unpack_chunk(h, part):
        p = 2 * h + part
        arrived(5 + p, r_ret, p * 512)
        for sig in range(2):
            for a in range(4):
                for c in range(2):
                    t_ret[
                        pl.ds(((h * 2 + sig) * 4 + a) * LANES + 64 * part + c, 32, stride=2), :
                    ] = r_ret[pl.ds(p * 512 + a * 4 + sig * 2 + c, 32, stride=16), :]

    stores = []

    def finish(h):
        c = pl.ds(LANES * h, LANES)
        for a in range(4):
            p = pl.ds(LANES * a, LANES)
            conv = t_ret[pl.ds(((h * 2 + 0) * 4 + a) * LANES, LANES), :].T
            adj = t_ret[pl.ds(((h * 2 + 1) * 4 + a) * LANES, LANES), :].T
            o_query[0, p, c] = (grad[0, p, c].astype(F32) * conv).astype(BF)
            o_key[0, p, c] = (adj * value[0, p, c].astype(F32)).astype(BF)
            o_value[0, p, c] = (adj * key_in[0, p, c].astype(F32)).astype(BF)
        for i, (src, dst) in enumerate(
            ((o_query, out_query), (o_key, out_key), (o_value, out_value))
        ):
            store = pltpu.make_async_copy(src.at[:, :, c], dst.at[:, :, c], store_sem.at[2 * i + h])
            store.start()
            stores.append(store)

    own_taps = r_taps.at[pl.ds(pl.multiple_of(odd * 512, 512), 512)]
    other_taps = r_taps.at[pl.ds(pl.multiple_of((1 - odd) * 512, 512), 512)]
    loads[0].wait()
    loads[1].wait()
    loads[2].wait()
    loads[3].wait()
    transpose_gd(0)
    pack_gd(0)
    pl.semaphore_wait(barrier, SEQ + DP - 2)
    exchange(0, s_gd, r_gd, 0)
    loads[4].wait()
    pack_taps()
    exchange(4, s_taps, own_taps, 0)
    pack_gd(1)
    exchange(1, s_gd, r_gd, 512)
    transpose_gd(1)
    pack_gd(2)
    exchange(2, s_gd, r_gd, 1024)
    pack_gd(3)
    loads[5].wait()
    loads[6].wait()

    arrived(0, r_gd, 0)
    gate_chunk(0)
    exchange(3, s_gd, r_gd, 1536)

    arrived(4, own_taps, 0)
    pair = pltpu.make_async_remote_copy(
        src_ref=own_taps,
        dst_ref=own_taps,
        send_sem=pair_send,
        recv_sem=pair_recv,
        device_id=(mate, me, tp),
        device_id_type=MESH,
    )
    pair.start()
    forward_taps(odd)

    arrived(1, r_gd, 512)
    gate_chunk(1)
    sum_chunk(0)
    return_chunk(odd)

    arrived(2, r_gd, 1024)
    gate_chunk(2)
    sum_chunk(1)
    pltpu.make_async_copy(other_taps, other_taps, pair_recv).wait()
    forward_taps(1 - odd)
    return_chunk(1 - odd)

    arrived(3, r_gd, 1536)
    gate_chunk(3)
    sum_chunk(2)
    spread_chunk(0)
    return_chunk(2 + odd)
    spread_chunk(1)
    return_chunk(3 - odd)
    sum_chunk(3)
    unpack_chunk(0, odd)
    spread_chunk(2)
    unpack_chunk(0, 1 - odd)
    finish(0)
    spread_chunk(3)
    unpack_chunk(1, odd)
    unpack_chunk(1, 1 - odd)
    finish(1)

    for p in range(4):
        part = z_all.at[pl.ds(0, DP - 1), :, pl.ds(2 * p, 2)]
        pltpu.make_async_copy(part, part, ag_recv.at[p]).wait()
        for a in range(4):
            for c in range(2):
                t_filt[
                    pl.ds(((p // 2) * 4 + a) * LANES + 64 * (p % 2) + c, 32, stride=2), :
                ] = z_all[a, :, 2 * p + c, :]
    for h in range(2):
        for a in range(4):
            o_filter[pl.ds(LANES * a, LANES), pl.ds(LANES * h, LANES)] = t_filt[
                pl.ds((h * 4 + a) * LANES, LANES), :
            ].T
    store = pltpu.make_async_copy(o_filter, out_filter, store_sem.at[6])
    store.start()
    stores.append(store)

    pair.wait_send()
    for index in range(9):
        part = s_gd.at[pl.ds(0, 496)]
        pltpu.make_async_copy(part, part, x_send.at[index]).wait()
    for p in range(4):
        part = z_sum.at[pl.ds(0, SEQ - 1), pl.ds(0, 2)]
        pltpu.make_async_copy(part, part, m_send.at[p]).wait()
        part = z_part.at[pl.ds(0, 192)]
        pltpu.make_async_copy(part, part, rs_send.at[p]).wait()
        part = z_all.at[pl.ds(0, DP - 1), :, pl.ds(0, 2)]
        pltpu.make_async_copy(part, part, ag_send.at[p]).wait()
    for store in stores:
        store.wait()


def shards(query, key_in, value, grad_out, filter_taps):
    tables = tuple(jnp.asarray(t) for t in make_tables())
    operands = (query, key_in, value, grad_out, filter_taps, *tables)
    results = (
        jax.ShapeDtypeStruct(query.shape, BF),
        jax.ShapeDtypeStruct(query.shape, BF),
        jax.ShapeDtypeStruct(query.shape, BF),
        jax.ShapeDtypeStruct(filter_taps.shape, F32),
    )

    def block(rows, lanes=LANES):
        return pltpu.VMEM((rows, lanes), F32)

    return pl.pallas_call(
        kernel,
        out_shape=results,
        in_specs=[pl.BlockSpec(memory_space=pl.ANY)] * 7,
        out_specs=(pl.BlockSpec(memory_space=pl.ANY),) * 4,
        scratch_shapes=[pltpu.VMEM(x.shape, x.dtype) for x in operands + results]
        + [block(2048), block(1024), block(1024), block(2048), block(1024)]
        + [block(2048), block(2048), block(512), block(1024), block(2048), block(2048)]
        + [block(2048, 2 * LANES), block(1024, 2 * LANES), block(1024), block(768)]
        + [pltpu.VMEM((SEQ, 8, LANES), F32), pltpu.VMEM((DP, SEQ, 8, LANES), F32)]
        + [pltpu.SemaphoreType.DMA((n,)) for n in (9, 9, 4, 4, 4, 4, 4, 4)]
        + [pltpu.SemaphoreType.DMA] * 2
        + [pltpu.SemaphoreType.DMA((7,)), pltpu.SemaphoreType.DMA((7,))],
        compiler_params=pltpu.CompilerParams(
            collective_id=0, has_side_effects=True, vmem_limit_bytes=60 * 1024 * 1024
        ),
    )(*operands)


def solution(mesh):
    wide = P("dp", "seq", "tp")
    narrow = P("seq", "tp")
    return jax.shard_map(
        shards,
        mesh=mesh,
        in_specs=(wide, wide, wide, wide, narrow),
        out_specs=(wide, wide, wide, narrow),
        check_vma=False,
    )
```

```python
import functools
import math

import jax
import jax.numpy as jnp
import ml_dtypes
import numpy as np
from jax import lax
from jax.experimental import pallas as pl
from jax.experimental.pallas import tpu as pltpu
from jax.sharding import PartitionSpec as P

MESH = pl.DeviceIdType.MESH
SEQ = 32
DP = 4
LANES = 128
ROWS = 1024
POINTS = 16384
BF = jnp.bfloat16
F32 = jnp.float32


def halves(table):
    table = np.asarray(table, np.float32)
    high = table.astype(ml_dtypes.bfloat16)
    low = (table - high.astype(np.float32)).astype(ml_dtypes.bfloat16)
    return high, low


def make_tables():
    idx = np.arange(LANES, dtype=np.float64)
    turn = 2.0 * math.pi * np.outer(idx + 0.25, idx) / LANES
    first = np.concatenate([np.cos(turn), -np.sin(turn)], axis=0)
    twist = 2.0 * math.pi * np.outer(idx + 0.25, idx) / POINTS
    plain = 2.0 * math.pi * np.outer(idx, idx) / LANES
    cos, sin = np.cos(plain), np.sin(plain)
    second = np.block([[cos, -sin], [sin, cos]])
    back = np.block([[cos, sin], [-sin, cos]])
    last = np.concatenate([np.cos(turn).T, -np.sin(turn).T], axis=1) / POINTS
    first_h, first_l = halves(first)
    mats = [
        np.concatenate([first_h, first_h], axis=1),
        np.concatenate([first_l, np.zeros_like(first_l)], axis=1),
        *halves(second),
        *halves(back),
        *halves(last),
    ]
    turns = [np.cos(twist), -np.sin(twist)]
    return np.concatenate(mats, axis=0), np.concatenate(turns, axis=0).astype(np.float32)


def split(x):
    high = x.astype(BF)
    return high, (x - high.astype(F32)).astype(BF)


def dot(a, b):
    return jnp.dot(a, b, preferred_element_type=F32)


def kernel(
    query_in, key_hbm, value_in, grad_in, taps_in, mats_in, turns_in,
    out_query, out_key, out_value, out_filter,
    query, key_in, value, grad, taps, mats, turns,
    o_query, o_key, o_value, o_filter,
    t_gd, t_taps, t_corr, t_ret, t_filt,
    s_gd, r_gd, s_taps, r_taps, s_ret, r_ret,
    f_gd, f_taps, c_part, z_part, z_sum, z_all,
    x_send, x_recv, m_send, m_recv, rs_send, rs_recv, ag_send, ag_recv,
    pair_send, pair_recv, load_sem, store_sem,
):
    dp = lax.axis_index("dp")
    me = lax.axis_index("seq")
    tp = lax.axis_index("tp")
    chip, core = me // 2, lax.rem(me, 2)
    x_at, y_at = chip // 4, lax.rem(chip, 4)
    odd = lax.rem(dp, 2)
    mate = dp + 1 - 2 * odd

    loads = [
        pltpu.make_async_copy(src, dst, load_sem.at[i])
        for i, (src, dst) in enumerate(
            (
                (key_hbm, key_in),
                (value_in, value),
                (grad_in, grad),
                (query_in, query),
                (taps_in, taps),
                (mats_in, mats),
                (turns_in, turns),
            )
        )
    ]
    for load in loads:
        load.start()
    first_cat = mats.at[pl.ds(0, 256)]
    first_l = mats.at[pl.ds(256, 256), pl.ds(0, LANES)]
    second_h, second_l, back_h, back_l = (mats.at[pl.ds(512 + 256 * i, 256)] for i in range(4))
    last_h, last_l = (mats.at[pl.ds(1536 + LANES * i, LANES)] for i in range(2))
    turn_re, turn_im = (turns.at[pl.ds(LANES * i, LANES)] for i in range(2))

    at_x = [lax.rem(x_at + d, 4) * 8 for d in (2, 3, 1, 0)]
    at_y = [lax.rem(y_at + d, 4) * 2 for d in (2, 3, 1, 0)]
    at_core = [1 - core, core]
    partners = [x + y + c for c in at_core for x in at_x for y in at_y][:-1]

    barrier = pltpu.get_barrier_semaphore()

    for to in partners:
        pl.semaphore_signal(barrier, inc=1, device_id=(dp, to, tp), device_id_type=MESH)

    for step in range(1, DP):
        pl.semaphore_signal(
            barrier, inc=1, device_id=(lax.rem(dp + step, DP), me, tp), device_id_type=MESH
        )


    def exchange(index, src, dst, base):
        mine = pl.ds(pl.multiple_of(base + me * 16, 16), 16)

        for to in partners:
            pltpu.make_async_remote_copy(
                src_ref=src.at[pl.ds(pl.multiple_of(base + to * 16, 16), 16)],
                dst_ref=dst.at[mine],
                send_sem=x_send.at[index],
                recv_sem=x_recv.at[index],
                device_id=(dp, to, tp),
                device_id_type=MESH,
            ).start()

        pltpu.make_async_copy(src.at[mine], dst.at[mine], x_recv.at[index]).start()

    def arrived(index, dst, base):
        part = dst.at[pl.ds(pl.multiple_of(base, 512), 512)]
        pltpu.make_async_copy(part, part, x_recv.at[index]).wait()


    def transpose_gd(h):
        c = pl.ds(LANES * h, LANES)
        for sig, (left, right) in enumerate(((key_in, value), (grad, query))):
            for a in range(4):
                p = pl.ds(LANES * a, LANES)
                at = ((h * 2 + sig) * 4 + a) * LANES
                t_gd[pl.ds(at, LANES), :] = (left[0, p, c].astype(F32) * right[0, p, c].astype(F32)).T

    def pack_gd(p):
        for sig in range(2):
            for a in range(4):
                at = (((p // 2) * 2 + sig) * 4 + a) * LANES + 64 * (p % 2)
                for c in range(2):
                    s_gd[pl.ds(p * 512 + a * 4 + sig * 2 + c, 32, stride=16), :] = t_gd[
                        pl.ds(at + c, 32, stride=2), :
                    ]

    def pack_taps():
        for h in range(2):
            for a in range(4):
                at = (h * 4 + a) * LANES
                t_taps[pl.ds(at, LANES), :] = taps[pl.ds(LANES * a, LANES), pl.ds(LANES * h, LANES)].T
        for h in range(2):
            for a in range(4):
                at = (h * 4 + a) * LANES
                for c in range(2):
                    s_taps[pl.ds(a * 4 + h * 2 + c, 32, stride=16), :] = t_taps[
                        pl.ds(at + 64 * odd + c, 32, stride=2), :
                    ]


    def forward(src, base):
        y = jnp.concatenate([src[pl.ds(base + j, LANES, stride=4), :] for j in range(2)], axis=1)
        yh, yl = split(y)
        a = dot(first_cat[...], jnp.concatenate([yh, yl], axis=0)) + dot(first_l[...], yh)
        wr, wi = turn_re[...], turn_im[...]
        rows = []
        for j in range(2):
            re, im = a[:LANES, LANES * j : LANES * (j + 1)], a[LANES:, LANES * j : LANES * (j + 1)]
            rows.append(jnp.concatenate([re * wr - im * wi, re * wi + im * wr], axis=1))
        ph, pw = split(jnp.concatenate(rows, axis=0))
        return dot(ph, second_h[...]) + dot(pw, second_h[...]) + dot(ph, second_l[...])

    def inverse(left, right, conj):
        lr, li, rr, ri = left[:, :LANES], left[:, LANES:], right[:, :LANES], right[:, LANES:]
        if conj:
            prod = [lr * rr + li * ri, lr * ri - li * rr]
        else:
            prod = [lr * rr - li * ri, lr * ri + li * rr]
        ph, pw = split(jnp.concatenate(prod, axis=1))
        b = dot(ph, back_h[...]) + dot(pw, back_h[...]) + dot(ph, back_l[...])
        wr, wi = turn_re[...], turn_im[...]
        cols = []
        for j in range(2):
            re, im = b[LANES * j : LANES * (j + 1), :LANES], b[LANES * j : LANES * (j + 1), LANES:]
            cols.append(jnp.concatenate([re * wr + im * wi, im * wr - re * wi], axis=0))
        zh, zl = split(jnp.concatenate(cols, axis=1))
        return dot(last_h[...], zh) + dot(last_h[...], zl) + dot(last_l[...], zh)

    def spec_at(p, sig):
        return pl.ds(pl.multiple_of((p * 2 + sig) * 256, 256), 256)

    def gate_chunk(p):
        gate = forward(r_gd, p * 512)
        dgate = forward(r_gd, p * 512 + 2)
        f_gd[spec_at(p, 0), :] = gate
        f_gd[spec_at(p, 1), :] = dgate
        y = inverse(gate, dgate, True)
        for c in range(2):
            at = (p * 2 + c) * LANES
            t_corr[pl.ds(at, LANES), :] = y[:, LANES * c : LANES * (c + 1)]
            for a in range(4):
                c_part[pl.ds(p * 256 + a * 64 + c, 32, stride=2), :] = t_corr[
                    pl.ds(at + a, 32, stride=4), :
                ]
        for step in range(1, DP):
            to = lax.rem(dp + step, DP)
            pltpu.make_async_remote_copy(
                src_ref=c_part.at[pl.ds(pl.multiple_of(p * 256 + to * 64, 64), 64)],
                dst_ref=z_part.at[pl.ds((p * 3 + step - 1) * 64, 64)],
                send_sem=rs_send.at[p],
                recv_sem=rs_recv.at[p],
                device_id=(to, me, tp),
                device_id_type=MESH,
            ).start()

    def sum_chunk(p):
        part = z_part.at[pl.ds(p * 192, 192)]
        pltpu.make_async_copy(part, part, rs_recv.at[p]).wait()
        scale = 1.0 / math.sqrt(DP * POINTS)
        for c in range(2):
            total = c_part[pl.ds(p * 256 + dp * 64 + c, 32, stride=2), :]
            for step in range(DP - 1):
                total = total + z_part[pl.ds((p * 3 + step) * 64 + c, 32, stride=2), :]
            z_sum[:, 2 * p + c, :] = total * scale
        two = pl.ds(2 * p, 2)

        for to in partners:
            pltpu.make_async_remote_copy(
                src_ref=z_sum.at[to, two],
                dst_ref=z_all.at[dp, me, two],
                send_sem=m_send.at[p],
                recv_sem=m_recv.at[p],
                device_id=(dp, to, tp),
                device_id_type=MESH,
            ).start()

        pltpu.make_async_copy(z_sum.at[me, two], z_all.at[dp, me, two], m_recv.at[p]).start()

    def spread_chunk(p):
        part = z_all.at[dp, :, pl.ds(2 * p, 2)]
        pltpu.make_async_copy(part, part, m_recv.at[p]).wait()
        for step in range(1, DP):
            pltpu.make_async_remote_copy(
                src_ref=part,
                dst_ref=part,
                send_sem=ag_send.at[p],
                recv_sem=ag_recv.at[p],
                device_id=(lax.rem(dp + step, DP), me, tp),
                device_id_type=MESH,
            ).start()

    def forward_taps(half):
        base = pl.multiple_of(half * 512, 512)
        for h in range(2):
            f_taps[pl.ds(pl.multiple_of((2 * h + half) * 256, 256), 256), :] = forward(
                r_taps, base + 2 * h
            )

    def return_chunk(p):
        filt = f_taps[pl.ds(pl.multiple_of(p * 256, 256), 256), :]
        conv = inverse(filt, f_gd[spec_at(p, 0), :], False)
        adj = inverse(filt, f_gd[spec_at(p, 1), :], True)
        for v in range(4):
            y = (conv, adj)[v // 2]
            s_ret[pl.ds(p * 512 + v, LANES, stride=4), :] = y[:, LANES * (v % 2) : LANES * (v % 2 + 1)]

    def send_chunk(p):
        exchange(5 + p, s_ret, r_ret, p * 512)

    def unpack_chunk(h, part):
        p = 2 * h + part
        arrived(5 + p, r_ret, p * 512)
        for sig in range(2):
            for a in range(4):
                for c in range(2):
                    t_ret[
                        pl.ds(((h * 2 + sig) * 4 + a) * LANES + 64 * part + c, 32, stride=2), :
                    ] = r_ret[pl.ds(p * 512 + a * 4 + sig * 2 + c, 32, stride=16), :]

    def finish(h):
        c = pl.ds(LANES * h, LANES)
        for a in range(4):
            p = pl.ds(LANES * a, LANES)
            conv = t_ret[pl.ds(((h * 2 + 0) * 4 + a) * LANES, LANES), :].T
            adj = t_ret[pl.ds(((h * 2 + 1) * 4 + a) * LANES, LANES), :].T
            o_query[0, p, c] = (grad[0, p, c].astype(F32) * conv).astype(BF)
            o_key[0, p, c] = (adj * value[0, p, c].astype(F32)).astype(BF)
            o_value[0, p, c] = (adj * key_in[0, p, c].astype(F32)).astype(BF)
        for i, (src, dst) in enumerate(
            ((o_query, out_query), (o_key, out_key), (o_value, out_value))
        ):
            store = pltpu.make_async_copy(src.at[:, :, c], dst.at[:, :, c], store_sem.at[2 * i + h])
            store.start()
            stores.append(store)

    stores = []
    own_taps = r_taps.at[pl.ds(pl.multiple_of(odd * 512, 512), 512)]
    other_taps = r_taps.at[pl.ds(pl.multiple_of((1 - odd) * 512, 512), 512)]
    loads[0].wait()
    loads[1].wait()
    loads[2].wait()
    loads[3].wait()
    transpose_gd(0)
    pack_gd(0)
    pl.semaphore_wait(barrier, SEQ + DP - 2)
    exchange(0, s_gd, r_gd, 0)
    loads[4].wait()
    pack_taps()
    exchange(4, s_taps, own_taps, 0)
    pack_gd(1)
    exchange(1, s_gd, r_gd, 512)
    transpose_gd(1)
    pack_gd(2)
    exchange(2, s_gd, r_gd, 1024)
    pack_gd(3)
    exchange(3, s_gd, r_gd, 1536)
    loads[5].wait()
    loads[6].wait()
    arrived(0, r_gd, 0)
    gate_chunk(0)
    arrived(4, own_taps, 0)
    pair = pltpu.make_async_remote_copy(
        src_ref=own_taps,
        dst_ref=own_taps,
        send_sem=pair_send,
        recv_sem=pair_recv,
        device_id=(mate, me, tp),
        device_id_type=MESH,
    )
    pair.start()
    forward_taps(odd)
    arrived(1, r_gd, 512)
    gate_chunk(1)
    return_chunk(odd)
    send_chunk(odd)
    sum_chunk(0)
    arrived(2, r_gd, 1024)
    gate_chunk(2)
    pltpu.make_async_copy(other_taps, other_taps, pair_recv).wait()
    forward_taps(1 - odd)
    return_chunk(1 - odd)
    send_chunk(1 - odd)
    sum_chunk(1)
    spread_chunk(0)
    arrived(3, r_gd, 1536)
    gate_chunk(3)
    return_chunk(2 + odd)
    send_chunk(2 + odd)
    sum_chunk(2)
    spread_chunk(1)
    return_chunk(3 - odd)
    sum_chunk(3)
    send_chunk(3 - odd)
    spread_chunk(2)
    unpack_chunk(0, odd)
    unpack_chunk(0, 1 - odd)
    finish(0)
    spread_chunk(3)
    unpack_chunk(1, odd)
    unpack_chunk(1, 1 - odd)
    finish(1)

    for p in range(4):
        part = z_all.at[pl.ds(0, DP - 1), :, pl.ds(2 * p, 2)]
        pltpu.make_async_copy(part, part, ag_recv.at[p]).wait()
        for a in range(4):
            for c in range(2):
                t_filt[
                    pl.ds(((p // 2) * 4 + a) * LANES + 64 * (p % 2) + c, 32, stride=2), :
                ] = z_all[a, :, 2 * p + c, :]
    for h in range(2):
        for a in range(4):
            o_filter[pl.ds(LANES * a, LANES), pl.ds(LANES * h, LANES)] = t_filt[
                pl.ds((h * 4 + a) * LANES, LANES), :
            ].T

    store = pltpu.make_async_copy(o_filter, out_filter, store_sem.at[6])
    store.start()
    stores.append(store)

    pair.wait_send()
    for index in range(9):
        part = s_gd.at[pl.ds(0, 496)]
        pltpu.make_async_copy(part, part, x_send.at[index]).wait()
    for p in range(4):
        part = z_sum.at[pl.ds(0, SEQ - 1), pl.ds(0, 2)]
        pltpu.make_async_copy(part, part, m_send.at[p]).wait()
        part = z_part.at[pl.ds(0, 192)]
        pltpu.make_async_copy(part, part, rs_send.at[p]).wait()
        part = z_all.at[pl.ds(0, DP - 1), :, pl.ds(0, 2)]
        pltpu.make_async_copy(part, part, ag_send.at[p]).wait()
    for store in stores:
        store.wait()


def store_kernel(*refs):
    ins, outs, held = refs[:4], refs[4:8], refs[8:12]
    loads = [pltpu.make_async_copy(ins[i], held[i], refs[12].at[i]) for i in range(4)]
    stores = [pltpu.make_async_copy(held[i], outs[i], refs[13].at[i]) for i in range(4)]
    for load in loads:
        load.start()
    for load, store in zip(loads, stores):
        load.wait()
        store.start()
    for store in stores:
        store.wait()


def shards(query, key_in, value, grad_out, filter_taps):
    tables = tuple(jnp.asarray(t) for t in make_tables())
    operands = (query, key_in, value, grad_out, filter_taps, *tables)
    results = (
        jax.ShapeDtypeStruct(query.shape, BF),
        jax.ShapeDtypeStruct(query.shape, BF),
        jax.ShapeDtypeStruct(query.shape, BF),
        jax.ShapeDtypeStruct(filter_taps.shape, F32),
    )

    def block(rows, lanes=LANES):
        return pltpu.VMEM((rows, lanes), F32)

    outs = pl.pallas_call(
        kernel,
        out_shape=results,
        in_specs=[pl.BlockSpec(memory_space=pl.ANY)] * 7,
        out_specs=(pl.BlockSpec(memory_space=pl.ANY),) * 4,
        scratch_shapes=[pltpu.VMEM(x.shape, x.dtype) for x in operands + results]
        + [block(2048), block(1024), block(1024), block(2048), block(1024)]
        + [block(2048), block(2048), block(512), block(1024), block(2048), block(2048)]
        + [block(2048, 2 * LANES), block(1024, 2 * LANES), block(1024), block(768)]
        + [pltpu.VMEM((SEQ, 8, LANES), F32), pltpu.VMEM((DP, SEQ, 8, LANES), F32)]
        + [pltpu.SemaphoreType.DMA((n,)) for n in (9, 9, 4, 4, 4, 4, 4, 4)]
        + [pltpu.SemaphoreType.DMA] * 2
        + [pltpu.SemaphoreType.DMA((7,)), pltpu.SemaphoreType.DMA((7,))],
        compiler_params=pltpu.CompilerParams(
            collective_id=0, has_side_effects=True, vmem_limit_bytes=61 * 1024 * 1024
        ),
    )(*operands)
    return pl.pallas_call(
        store_kernel,
        out_shape=results,
        in_specs=[pl.BlockSpec(memory_space=pl.ANY)] * 4,
        out_specs=(pl.BlockSpec(memory_space=pl.ANY),) * 4,
        scratch_shapes=[pltpu.VMEM(x.shape, x.dtype) for x in results]
        + [pltpu.SemaphoreType.DMA((4,))] * 2,
        compiler_params=pltpu.CompilerParams(
            has_side_effects=True, vmem_limit_bytes=61 * 1024 * 1024
        ),
    )(*outs)


def solution(mesh):
    wide = P("dp", "seq", "tp")
    narrow = P("seq", "tp")
    return jax.shard_map(
        shards,
        mesh=mesh,
        in_specs=(wide, wide, wide, wide, narrow),
        out_specs=(wide, wide, wide, narrow),
        check_vma=False,
    )
```

```python
import functools
import math

import jax
import jax.numpy as jnp
import ml_dtypes
import numpy as np
from jax import lax
from jax.experimental import pallas as pl
from jax.experimental.pallas import tpu as pltpu
from jax.sharding import PartitionSpec as P

MESH = pl.DeviceIdType.MESH
SEQ = 32
DP = 4
LANES = 128
ROWS = 1024
POINTS = 16384
BF = jnp.bfloat16
F32 = jnp.float32


def halves(table):
    table = np.asarray(table, np.float32)
    high = table.astype(ml_dtypes.bfloat16)
    low = (table - high.astype(np.float32)).astype(ml_dtypes.bfloat16)
    return high, low


def make_tables():
    idx = np.arange(LANES, dtype=np.float64)
    turn = 2.0 * math.pi * np.outer(idx + 0.25, idx) / LANES
    first = np.concatenate([np.cos(turn), -np.sin(turn)], axis=0)
    twist = 2.0 * math.pi * np.outer(idx + 0.25, idx) / POINTS
    plain = 2.0 * math.pi * np.outer(idx, idx) / LANES
    cos, sin = np.cos(plain), np.sin(plain)
    second = np.block([[cos, -sin], [sin, cos]])
    back = np.block([[cos, sin], [-sin, cos]])
    last = np.concatenate([np.cos(turn).T, -np.sin(turn).T], axis=1) / POINTS
    first_h, first_l = halves(first)
    mats = [
        np.concatenate([first_h, first_h], axis=1),
        np.concatenate([first_l, np.zeros_like(first_l)], axis=1),
        *halves(second),
        *halves(back),
        *halves(last),
    ]
    turns = [np.cos(twist), -np.sin(twist)]
    return np.concatenate(mats, axis=0), np.concatenate(turns, axis=0).astype(np.float32)


def split(x):
    high = x.astype(BF)
    return high, (x - high.astype(F32)).astype(BF)


def dot(a, b):
    return jnp.dot(a, b, preferred_element_type=F32)


def kernel(
    query_in, key_hbm, value_in, grad_in, taps_in, mats_in, turns_in,
    out_query, out_key, out_value, out_filter,
    query, key_in, value, grad, taps, mats, turns,
    o_query, o_key, o_value, o_filter,
    t_gd, t_taps, t_corr, t_ret, t_filt,
    s_gd, r_gd, s_taps, r_taps, s_ret, r_ret,
    f_gd, f_taps, c_part, z_part, z_sum, z_all,
    x_send, x_recv, m_send, m_recv, rs_send, rs_recv, ag_send, ag_recv,
    load_sem, store_sem,
):
    dp = lax.axis_index("dp")
    me = lax.axis_index("seq")
    tp = lax.axis_index("tp")
    chip, core = me // 2, lax.rem(me, 2)
    x_at, y_at = chip // 4, lax.rem(chip, 4)

    loads = [
        pltpu.make_async_copy(src, dst, load_sem.at[i])
        for i, (src, dst) in enumerate(
            (
                (key_hbm, key_in),
                (value_in, value),
                (grad_in, grad),
                (query_in, query),
                (taps_in, taps),
                (mats_in, mats),
                (turns_in, turns),
            )
        )
    ]
    for load in loads:
        load.start()
    first_cat = mats.at[pl.ds(0, 256)]
    first_l = mats.at[pl.ds(256, 256), pl.ds(0, LANES)]
    second_h, second_l, back_h, back_l = (mats.at[pl.ds(512 + 256 * i, 256)] for i in range(4))
    last_h, last_l = (mats.at[pl.ds(1536 + LANES * i, LANES)] for i in range(2))
    turn_re, turn_im = (turns.at[pl.ds(LANES * i, LANES)] for i in range(2))

    at_x = [lax.rem(x_at + d, 4) * 8 for d in (2, 3, 1, 0)]
    at_y = [lax.rem(y_at + d, 4) * 2 for d in (2, 3, 1, 0)]
    at_core = [1 - core, core]
    partners = [x + y + c for c in at_core for x in at_x for y in at_y][:-1]

    barrier = pltpu.get_barrier_semaphore()

    for to in partners:
        pl.semaphore_signal(barrier, inc=1, device_id=(dp, to, tp), device_id_type=MESH)

    for step in range(1, DP):
        pl.semaphore_signal(
            barrier, inc=1, device_id=(lax.rem(dp + step, DP), me, tp), device_id_type=MESH
        )


    def exchange(index, src, dst, base):
        mine = pl.ds(pl.multiple_of(base + me * 16, 16), 16)

        for to in partners:
            pltpu.make_async_remote_copy(
                src_ref=src.at[pl.ds(pl.multiple_of(base + to * 16, 16), 16)],
                dst_ref=dst.at[mine],
                send_sem=x_send.at[index],
                recv_sem=x_recv.at[index],
                device_id=(dp, to, tp),
                device_id_type=MESH,
            ).start()

        pltpu.make_async_copy(src.at[mine], dst.at[mine], x_recv.at[index]).start()

    def arrived(index, dst, base):
        part = dst.at[pl.ds(base, 512)]
        pltpu.make_async_copy(part, part, x_recv.at[index]).wait()


    def transpose_gd(h):
        c = pl.ds(LANES * h, LANES)
        for sig, (left, right) in enumerate(((key_in, value), (grad, query))):
            for a in range(4):
                p = pl.ds(LANES * a, LANES)
                at = ((h * 2 + sig) * 4 + a) * LANES
                t_gd[pl.ds(at, LANES), :] = (left[0, p, c].astype(F32) * right[0, p, c].astype(F32)).T

    def pack_gd(p):
        for sig in range(2):
            for a in range(4):
                at = (((p // 2) * 2 + sig) * 4 + a) * LANES + 64 * (p % 2)
                for c in range(2):
                    s_gd[pl.ds(p * 512 + a * 4 + sig * 2 + c, 32, stride=16), :] = t_gd[
                        pl.ds(at + c, 32, stride=2), :
                    ]

    def pack_taps(h):
        for a in range(4):
            at = (h * 4 + a) * LANES
            t_taps[pl.ds(at, LANES), :] = taps[pl.ds(LANES * a, LANES), pl.ds(LANES * h, LANES)].T
            for v in range(4):
                s_taps[pl.ds(h * 512 + a * 4 + v, 32, stride=16), :] = t_taps[
                    pl.ds(at + 64 * (v // 2) + v % 2, 32, stride=2), :
                ]


    def forward(src, base):
        y = jnp.concatenate([src[pl.ds(base + j, LANES, stride=4), :] for j in range(2)], axis=1)
        yh, yl = split(y)
        a = dot(first_cat[...], jnp.concatenate([yh, yl], axis=0)) + dot(first_l[...], yh)
        wr, wi = turn_re[...], turn_im[...]
        rows = []
        for j in range(2):
            re, im = a[:LANES, LANES * j : LANES * (j + 1)], a[LANES:, LANES * j : LANES * (j + 1)]
            rows.append(jnp.concatenate([re * wr - im * wi, re * wi + im * wr], axis=1))
        ph, pw = split(jnp.concatenate(rows, axis=0))
        return dot(ph, second_h[...]) + dot(pw, second_h[...]) + dot(ph, second_l[...])

    def inverse(left, right, conj):
        lr, li, rr, ri = left[:, :LANES], left[:, LANES:], right[:, :LANES], right[:, LANES:]
        if conj:
            prod = [lr * rr + li * ri, lr * ri - li * rr]
        else:
            prod = [lr * rr - li * ri, lr * ri + li * rr]
        ph, pw = split(jnp.concatenate(prod, axis=1))
        b = dot(ph, back_h[...]) + dot(pw, back_h[...]) + dot(ph, back_l[...])
        wr, wi = turn_re[...], turn_im[...]
        cols = []
        for j in range(2):
            re, im = b[LANES * j : LANES * (j + 1), :LANES], b[LANES * j : LANES * (j + 1), LANES:]
            cols.append(jnp.concatenate([re * wr + im * wi, im * wr - re * wi], axis=0))
        zh, zl = split(jnp.concatenate(cols, axis=1))
        return dot(last_h[...], zh) + dot(last_h[...], zl) + dot(last_l[...], zh)

    def spec_at(p, sig):
        return pl.ds((p * 2 + sig) * 256, 256)

    def gate_chunk(p):
        gate = forward(r_gd, p * 512)
        dgate = forward(r_gd, p * 512 + 2)
        f_gd[spec_at(p, 0), :] = gate
        f_gd[spec_at(p, 1), :] = dgate
        y = inverse(gate, dgate, True)
        for c in range(2):
            at = (p * 2 + c) * LANES
            t_corr[pl.ds(at, LANES), :] = y[:, LANES * c : LANES * (c + 1)]
            for a in range(4):
                c_part[pl.ds(p * 256 + a * 64 + c, 32, stride=2), :] = t_corr[
                    pl.ds(at + a, 32, stride=4), :
                ]
        for step in range(1, DP):
            to = lax.rem(dp + step, DP)
            pltpu.make_async_remote_copy(
                src_ref=c_part.at[pl.ds(pl.multiple_of(p * 256 + to * 64, 64), 64)],
                dst_ref=z_part.at[pl.ds((p * 3 + step - 1) * 64, 64)],
                send_sem=rs_send.at[p],
                recv_sem=rs_recv.at[p],
                device_id=(to, me, tp),
                device_id_type=MESH,
            ).start()

    def sum_chunk(p):
        part = z_part.at[pl.ds(p * 192, 192)]
        pltpu.make_async_copy(part, part, rs_recv.at[p]).wait()
        scale = 1.0 / math.sqrt(DP * POINTS)
        for c in range(2):
            total = c_part[pl.ds(p * 256 + dp * 64 + c, 32, stride=2), :]
            for step in range(DP - 1):
                total = total + z_part[pl.ds((p * 3 + step) * 64 + c, 32, stride=2), :]
            z_sum[:, 2 * p + c, :] = total * scale
        two = pl.ds(2 * p, 2)

        for to in partners:
            pltpu.make_async_remote_copy(
                src_ref=z_sum.at[to, two],
                dst_ref=z_all.at[dp, me, two],
                send_sem=m_send.at[p],
                recv_sem=m_recv.at[p],
                device_id=(dp, to, tp),
                device_id_type=MESH,
            ).start()

        pltpu.make_async_copy(z_sum.at[me, two], z_all.at[dp, me, two], m_recv.at[p]).start()

    def spread_chunk(p):
        part = z_all.at[dp, :, pl.ds(2 * p, 2)]
        pltpu.make_async_copy(part, part, m_recv.at[p]).wait()
        for step in range(1, DP):
            pltpu.make_async_remote_copy(
                src_ref=part,
                dst_ref=part,
                send_sem=ag_send.at[p],
                recv_sem=ag_recv.at[p],
                device_id=(lax.rem(dp + step, DP), me, tp),
                device_id_type=MESH,
            ).start()

    def forward_taps(p):
        f_taps[pl.ds(p * 256, 256), :] = forward(r_taps, (p // 2) * 512 + 2 * (p % 2))

    def return_chunk(p):
        filt = f_taps[pl.ds(p * 256, 256), :]
        conv = inverse(filt, f_gd[spec_at(p, 0), :], False)
        adj = inverse(filt, f_gd[spec_at(p, 1), :], True)
        for v in range(4):
            y = (conv, adj)[v // 2]
            s_ret[pl.ds(p * 512 + v, LANES, stride=4), :] = y[:, LANES * (v % 2) : LANES * (v % 2 + 1)]

    def send_chunk(p):
        exchange(6 + p, s_ret, r_ret, p * 512)

    def unpack_chunk(p):
        arrived(6 + p, r_ret, p * 512)
        for sig in range(2):
            for a in range(4):
                at = (((p // 2) * 2 + sig) * 4 + a) * LANES + 64 * (p % 2)
                for c in range(2):
                    t_ret[pl.ds(at + c, 32, stride=2), :] = r_ret[
                        pl.ds(p * 512 + a * 4 + sig * 2 + c, 32, stride=16), :
                    ]

    def unpack_filter(p):
        part = z_all.at[pl.ds(0, DP - 1), :, pl.ds(2 * p, 2)]
        pltpu.make_async_copy(part, part, ag_recv.at[p]).wait()
        for a in range(4):
            at = ((p // 2) * 4 + a) * LANES + 64 * (p % 2)
            for c in range(2):
                t_filt[pl.ds(at + c, 32, stride=2), :] = z_all[a, :, 2 * p + c, :]

    def finish_filter(h):
        c = pl.ds(LANES * h, LANES)
        for a in range(4):
            o_filter[pl.ds(LANES * a, LANES), c] = t_filt[pl.ds((h * 4 + a) * LANES, LANES), :].T
        store = pltpu.make_async_copy(o_filter.at[:, c], out_filter.at[:, c], store_sem.at[6 + h])
        store.start()
        stores.append(store)

    def finish(h):
        c = pl.ds(LANES * h, LANES)
        for a in range(4):
            p = pl.ds(LANES * a, LANES)
            conv = t_ret[pl.ds(((h * 2 + 0) * 4 + a) * LANES, LANES), :].T
            adj = t_ret[pl.ds(((h * 2 + 1) * 4 + a) * LANES, LANES), :].T
            o_query[0, p, c] = (grad[0, p, c].astype(F32) * conv).astype(BF)
            o_key[0, p, c] = (adj * value[0, p, c].astype(F32)).astype(BF)
            o_value[0, p, c] = (adj * key_in[0, p, c].astype(F32)).astype(BF)
        for i, (src, dst) in enumerate(
            ((o_query, out_query), (o_key, out_key), (o_value, out_value))
        ):
            store = pltpu.make_async_copy(src.at[:, :, c], dst.at[:, :, c], store_sem.at[2 * i + h])
            store.start()
            stores.append(store)

    stores = []
    loads[0].wait()
    loads[1].wait()
    loads[2].wait()
    loads[3].wait()
    transpose_gd(0)
    pack_gd(0)
    pl.semaphore_wait(barrier, SEQ + DP - 2)
    exchange(0, s_gd, r_gd, 0)
    pack_gd(1)
    exchange(1, s_gd, r_gd, 512)
    loads[4].wait()
    pack_taps(0)
    exchange(4, s_taps, r_taps, 0)
    transpose_gd(1)
    pack_gd(2)
    exchange(2, s_gd, r_gd, 1024)
    pack_gd(3)
    loads[5].wait()
    loads[6].wait()
    arrived(0, r_gd, 0)
    gate_chunk(0)
    arrived(1, r_gd, 512)
    gate_chunk(1)
    sum_chunk(0)
    exchange(3, s_gd, r_gd, 1536)
    pack_taps(1)
    exchange(5, s_taps, r_taps, 512)
    arrived(4, r_taps, 0)
    forward_taps(0)
    forward_taps(1)
    return_chunk(0)
    send_chunk(0)
    arrived(2, r_gd, 1024)
    gate_chunk(2)
    sum_chunk(1)
    spread_chunk(0)
    return_chunk(1)
    send_chunk(1)
    arrived(3, r_gd, 1536)
    gate_chunk(3)
    sum_chunk(2)
    arrived(5, r_taps, 512)
    forward_taps(2)
    return_chunk(2)
    spread_chunk(1)
    forward_taps(3)
    sum_chunk(3)
    send_chunk(2)
    return_chunk(3)
    send_chunk(3)
    unpack_chunk(0)
    unpack_chunk(1)
    finish(0)
    spread_chunk(2)
    unpack_filter(0)
    spread_chunk(3)
    unpack_filter(1)
    finish_filter(0)
    unpack_chunk(2)
    unpack_chunk(3)
    finish(1)
    unpack_filter(2)
    unpack_filter(3)
    finish_filter(1)

    for index in range(10):
        part = s_gd.at[pl.ds(0, 496)]
        pltpu.make_async_copy(part, part, x_send.at[index]).wait()
    for p in range(4):
        part = z_sum.at[pl.ds(0, SEQ - 1), pl.ds(0, 2)]
        pltpu.make_async_copy(part, part, m_send.at[p]).wait()
        part = z_part.at[pl.ds(0, 192)]
        pltpu.make_async_copy(part, part, rs_send.at[p]).wait()
        part = z_all.at[pl.ds(0, DP - 1), :, pl.ds(0, 2)]
        pltpu.make_async_copy(part, part, ag_send.at[p]).wait()
    for store in stores:
        store.wait()


def store_kernel(*refs):
    ins, outs, held = refs[:4], refs[4:8], refs[8:12]
    loads = [pltpu.make_async_copy(ins[i], held[i], refs[12].at[i]) for i in range(4)]
    stores = [pltpu.make_async_copy(held[i], outs[i], refs[13].at[i]) for i in range(4)]
    for load in loads:
        load.start()
    for load, store in zip(loads, stores):
        load.wait()
        store.start()
    for store in stores:
        store.wait()


def shards(query, key_in, value, grad_out, filter_taps):
    tables = tuple(jnp.asarray(t) for t in make_tables())
    operands = (query, key_in, value, grad_out, filter_taps, *tables)
    results = (
        jax.ShapeDtypeStruct(query.shape, BF),
        jax.ShapeDtypeStruct(query.shape, BF),
        jax.ShapeDtypeStruct(query.shape, BF),
        jax.ShapeDtypeStruct(filter_taps.shape, F32),
    )

    def block(rows, lanes=LANES):
        return pltpu.VMEM((rows, lanes), F32)

    outs = pl.pallas_call(
        kernel,
        out_shape=results,
        in_specs=[pl.BlockSpec(memory_space=pl.ANY)] * 7,
        out_specs=(pl.BlockSpec(memory_space=pl.ANY),) * 4,
        scratch_shapes=[pltpu.VMEM(x.shape, x.dtype) for x in operands + results]
        + [block(2048), block(1024), block(1024), block(2048), block(1024)]
        + [block(2048), block(2048), block(1024), block(1024), block(2048), block(2048)]
        + [block(2048, 2 * LANES), block(1024, 2 * LANES), block(1024), block(768)]
        + [pltpu.VMEM((SEQ, 8, LANES), F32), pltpu.VMEM((DP, SEQ, 8, LANES), F32)]
        + [pltpu.SemaphoreType.DMA((n,)) for n in (10, 10, 4, 4, 4, 4, 4, 4)]
        + [pltpu.SemaphoreType.DMA((7,)), pltpu.SemaphoreType.DMA((8,))],
        compiler_params=pltpu.CompilerParams(
            collective_id=0, has_side_effects=True, vmem_limit_bytes=61 * 1024 * 1024
        ),
    )(*operands)
    return pl.pallas_call(
        store_kernel,
        out_shape=results,
        in_specs=[pl.BlockSpec(memory_space=pl.ANY)] * 4,
        out_specs=(pl.BlockSpec(memory_space=pl.ANY),) * 4,
        scratch_shapes=[pltpu.VMEM(x.shape, x.dtype) for x in results]
        + [pltpu.SemaphoreType.DMA((4,))] * 2,
        compiler_params=pltpu.CompilerParams(
            has_side_effects=True, vmem_limit_bytes=61 * 1024 * 1024
        ),
    )(*outs)


def solution(mesh):
    wide = P("dp", "seq", "tp")
    narrow = P("seq", "tp")
    return jax.shard_map(
        shards,
        mesh=mesh,
        in_specs=(wide, wide, wide, wide, narrow),
        out_specs=(wide, wide, wide, narrow),
        check_vma=False,
    )
```

```python
import functools
import math

import jax
import jax.numpy as jnp
import ml_dtypes
import numpy as np
from jax import lax
from jax.experimental import pallas as pl
from jax.experimental.pallas import tpu as pltpu
from jax.sharding import PartitionSpec as P

MESH = pl.DeviceIdType.MESH
SEQ = 32
DP = 4
LANES = 128
ROWS = 1024
POINTS = 16384
BF = jnp.bfloat16
F32 = jnp.float32


def halves(table):
    table = np.asarray(table, np.float32)
    high = table.astype(ml_dtypes.bfloat16)
    low = (table - high.astype(np.float32)).astype(ml_dtypes.bfloat16)
    return high, low


def make_tables():
    idx = np.arange(LANES, dtype=np.float64)
    turn = 2.0 * math.pi * np.outer(idx + 0.25, idx) / LANES
    first = np.concatenate([np.cos(turn), -np.sin(turn)], axis=0)
    twist = 2.0 * math.pi * np.outer(idx + 0.25, idx) / POINTS
    plain = 2.0 * math.pi * np.outer(idx, idx) / LANES
    cos, sin = np.cos(plain), np.sin(plain)
    second = np.block([[cos, -sin], [sin, cos]])
    back = np.block([[cos, sin], [-sin, cos]])
    last = np.concatenate([np.cos(turn).T, -np.sin(turn).T], axis=1) / POINTS
    first_h, first_l = halves(first)
    mats = [
        np.concatenate([first_h, first_h], axis=1),
        np.concatenate([first_l, np.zeros_like(first_l)], axis=1),
        *halves(second),
        *halves(back),
        *halves(last),
    ]
    turns = [np.cos(twist), -np.sin(twist)]
    return np.concatenate(mats, axis=0), np.concatenate(turns, axis=0).astype(np.float32)


def split(x):
    high = x.astype(BF)
    return high, (x - high.astype(F32)).astype(BF)


def dot(a, b):
    return jnp.dot(a, b, preferred_element_type=F32)


def kernel(
    query_in, key_hbm, value_in, grad_in, taps_in, mats_in, turns_in,
    out_query, out_key, out_value, out_filter,
    query, key_in, value, grad, taps, mats, turns,
    o_query, o_key, o_value, o_filter,
    t_gd, t_taps, t_corr, t_ret, t_filt,
    s_gd, r_gd, s_taps, r_taps, s_ret, r_ret,
    f_gd, f_taps, c_part, z_part, z_sum, z_all,
    x_send, x_recv, m_send, m_recv, rs_send, rs_recv, ag_send, ag_recv,
    load_sem, store_sem,
):
    dp = lax.axis_index("dp")
    me = lax.axis_index("seq")
    tp = lax.axis_index("tp")
    chip, core = me // 2, lax.rem(me, 2)
    x_at, y_at = chip // 4, lax.rem(chip, 4)

    loads = [
        pltpu.make_async_copy(src, dst, load_sem.at[i])
        for i, (src, dst) in enumerate(
            (
                (key_hbm, key_in),
                (value_in, value),
                (grad_in, grad),
                (query_in, query),
                (taps_in, taps),
                (mats_in, mats),
                (turns_in, turns),
            )
        )
    ]
    for load in loads:
        load.start()
    first_cat = mats.at[pl.ds(0, 256)]
    first_l = mats.at[pl.ds(256, 256), pl.ds(0, LANES)]
    second_h, second_l, back_h, back_l = (mats.at[pl.ds(512 + 256 * i, 256)] for i in range(4))
    last_h, last_l = (mats.at[pl.ds(1536 + LANES * i, LANES)] for i in range(2))
    turn_re, turn_im = (turns.at[pl.ds(LANES * i, LANES)] for i in range(2))

    at_x = [lax.rem(x_at + d, 4) * 8 for d in (2, 3, 1, 0)]
    at_y = [lax.rem(y_at + d, 4) * 2 for d in (2, 3, 1, 0)]
    at_core = [1 - core, core]
    partners = [x + y + c for c in at_core for x in at_x for y in at_y][:-1]

    barrier = pltpu.get_barrier_semaphore()

    for to in partners:
        pl.semaphore_signal(barrier, inc=1, device_id=(dp, to, tp), device_id_type=MESH)

    for step in range(1, DP):
        pl.semaphore_signal(
            barrier, inc=1, device_id=(lax.rem(dp + step, DP), me, tp), device_id_type=MESH
        )


    def exchange(index, src, dst, base):
        mine = pl.ds(pl.multiple_of(base + me * 16, 16), 16)

        for to in partners:
            pltpu.make_async_remote_copy(
                src_ref=src.at[pl.ds(pl.multiple_of(base + to * 16, 16), 16)],
                dst_ref=dst.at[mine],
                send_sem=x_send.at[index],
                recv_sem=x_recv.at[index],
                device_id=(dp, to, tp),
                device_id_type=MESH,
            ).start()

        pltpu.make_async_copy(src.at[mine], dst.at[mine], x_recv.at[index]).start()

    def arrived(index, dst, base):
        part = dst.at[pl.ds(base, 512)]
        pltpu.make_async_copy(part, part, x_recv.at[index]).wait()


    def transpose_gd(h):
        c = pl.ds(LANES * h, LANES)
        for sig, (left, right) in enumerate(((key_in, value), (grad, query))):
            for a in range(4):
                p = pl.ds(LANES * a, LANES)
                at = ((h * 2 + sig) * 4 + a) * LANES
                t_gd[pl.ds(at, LANES), :] = (left[0, p, c].astype(F32) * right[0, p, c].astype(F32)).T

    def pack_gd(p):
        for sig in range(2):
            for a in range(4):
                at = (((p // 2) * 2 + sig) * 4 + a) * LANES + 64 * (p % 2)
                for c in range(2):
                    s_gd[pl.ds(p * 512 + a * 4 + sig * 2 + c, 32, stride=16), :] = t_gd[
                        pl.ds(at + c, 32, stride=2), :
                    ]

    def pack_taps(h):
        for a in range(4):
            at = (h * 4 + a) * LANES
            t_taps[pl.ds(at, LANES), :] = taps[pl.ds(LANES * a, LANES), pl.ds(LANES * h, LANES)].T
            for v in range(4):
                s_taps[pl.ds(h * 512 + a * 4 + v, 32, stride=16), :] = t_taps[
                    pl.ds(at + 64 * (v // 2) + v % 2, 32, stride=2), :
                ]


    def forward(src, base):
        y = jnp.concatenate([src[pl.ds(base + j, LANES, stride=4), :] for j in range(2)], axis=1)
        yh, yl = split(y)
        a = dot(first_cat[...], jnp.concatenate([yh, yl], axis=0)) + dot(first_l[...], yh)
        wr, wi = turn_re[...], turn_im[...]
        rows = []
        for j in range(2):
            re, im = a[:LANES, LANES * j : LANES * (j + 1)], a[LANES:, LANES * j : LANES * (j + 1)]
            rows.append(jnp.concatenate([re * wr - im * wi, re * wi + im * wr], axis=1))
        ph, pw = split(jnp.concatenate(rows, axis=0))
        return dot(ph, second_h[...]) + dot(pw, second_h[...]) + dot(ph, second_l[...])

    def inverse(left, right, conj):
        lr, li, rr, ri = left[:, :LANES], left[:, LANES:], right[:, :LANES], right[:, LANES:]
        if conj:
            prod = [lr * rr + li * ri, lr * ri - li * rr]
        else:
            prod = [lr * rr - li * ri, lr * ri + li * rr]
        ph, pw = split(jnp.concatenate(prod, axis=1))
        b = dot(ph, back_h[...]) + dot(pw, back_h[...]) + dot(ph, back_l[...])
        wr, wi = turn_re[...], turn_im[...]
        cols = []
        for j in range(2):
            re, im = b[LANES * j : LANES * (j + 1), :LANES], b[LANES * j : LANES * (j + 1), LANES:]
            cols.append(jnp.concatenate([re * wr + im * wi, im * wr - re * wi], axis=0))
        zh, zl = split(jnp.concatenate(cols, axis=1))
        return dot(last_h[...], zh) + dot(last_h[...], zl) + dot(last_l[...], zh)

    def spec_at(p, sig):
        return pl.ds((p * 2 + sig) * 256, 256)

    def gate_chunk(p):
        gate = forward(r_gd, p * 512)
        dgate = forward(r_gd, p * 512 + 2)
        f_gd[spec_at(p, 0), :] = gate
        f_gd[spec_at(p, 1), :] = dgate
        y = inverse(gate, dgate, True)
        for c in range(2):
            at = (p * 2 + c) * LANES
            t_corr[pl.ds(at, LANES), :] = y[:, LANES * c : LANES * (c + 1)]
            for a in range(4):
                c_part[pl.ds(p * 256 + a * 64 + c, 32, stride=2), :] = t_corr[
                    pl.ds(at + a, 32, stride=4), :
                ]
        for step in range(1, DP):
            to = lax.rem(dp + step, DP)
            pltpu.make_async_remote_copy(
                src_ref=c_part.at[pl.ds(pl.multiple_of(p * 256 + to * 64, 64), 64)],
                dst_ref=z_part.at[pl.ds((p * 3 + step - 1) * 64, 64)],
                send_sem=rs_send.at[p],
                recv_sem=rs_recv.at[p],
                device_id=(to, me, tp),
                device_id_type=MESH,
            ).start()

    def sum_chunk(p):
        part = z_part.at[pl.ds(p * 192, 192)]
        pltpu.make_async_copy(part, part, rs_recv.at[p]).wait()
        scale = 1.0 / math.sqrt(DP * POINTS)
        for c in range(2):
            total = c_part[pl.ds(p * 256 + dp * 64 + c, 32, stride=2), :]
            for step in range(DP - 1):
                total = total + z_part[pl.ds((p * 3 + step) * 64 + c, 32, stride=2), :]
            z_sum[p, :, c, :] = total * scale

        for to in partners:
            pltpu.make_async_remote_copy(
                src_ref=z_sum.at[p, to],
                dst_ref=z_all.at[dp, p, me],
                send_sem=m_send.at[p],
                recv_sem=m_recv.at[p],
                device_id=(dp, to, tp),
                device_id_type=MESH,
            ).start()

        pltpu.make_async_copy(z_sum.at[p, me], z_all.at[dp, p, me], m_recv.at[p]).start()

    def spread_chunk(p):
        part = z_all.at[dp, p]
        pltpu.make_async_copy(part, part, m_recv.at[p]).wait()
        for step in range(1, DP):
            pltpu.make_async_remote_copy(
                src_ref=part,
                dst_ref=part,
                send_sem=ag_send.at[p],
                recv_sem=ag_recv.at[p],
                device_id=(lax.rem(dp + step, DP), me, tp),
                device_id_type=MESH,
            ).start()

    def forward_taps(p):
        f_taps[pl.ds(p * 256, 256), :] = forward(r_taps, (p // 2) * 512 + 2 * (p % 2))

    def return_chunk(p):
        filt = f_taps[pl.ds(p * 256, 256), :]
        conv = inverse(filt, f_gd[spec_at(p, 0), :], False)
        adj = inverse(filt, f_gd[spec_at(p, 1), :], True)
        for v in range(4):
            y = (conv, adj)[v // 2]
            s_ret[pl.ds(p * 512 + v, LANES, stride=4), :] = y[:, LANES * (v % 2) : LANES * (v % 2 + 1)]

    def send_chunk(p):
        exchange(6 + p, s_ret, r_ret, p * 512)

    def unpack_chunk(p):
        arrived(6 + p, r_ret, p * 512)
        for sig in range(2):
            for a in range(4):
                at = (((p // 2) * 2 + sig) * 4 + a) * LANES + 64 * (p % 2)
                for c in range(2):
                    t_ret[pl.ds(at + c, 32, stride=2), :] = r_ret[
                        pl.ds(p * 512 + a * 4 + sig * 2 + c, 32, stride=16), :
                    ]

    def unpack_filter(p):
        part = z_all.at[pl.ds(0, DP - 1), p]
        pltpu.make_async_copy(part, part, ag_recv.at[p]).wait()
        for a in range(4):
            at = ((p // 2) * 4 + a) * LANES + 64 * (p % 2)
            for c in range(2):
                t_filt[pl.ds(at + c, 32, stride=2), :] = z_all[a, p, :, c, :]

    def finish_filter(h):
        c = pl.ds(LANES * h, LANES)
        for a in range(4):
            o_filter[pl.ds(LANES * a, LANES), c] = t_filt[pl.ds((h * 4 + a) * LANES, LANES), :].T
        store = pltpu.make_async_copy(o_filter.at[:, c], out_filter.at[:, c], store_sem.at[6 + h])
        store.start()
        stores.append(store)

    def finish(h):
        c = pl.ds(LANES * h, LANES)
        for a in range(4):
            p = pl.ds(LANES * a, LANES)
            conv = t_ret[pl.ds(((h * 2 + 0) * 4 + a) * LANES, LANES), :].T
            adj = t_ret[pl.ds(((h * 2 + 1) * 4 + a) * LANES, LANES), :].T
            o_query[0, p, c] = (grad[0, p, c].astype(F32) * conv).astype(BF)
            o_key[0, p, c] = (adj * value[0, p, c].astype(F32)).astype(BF)
            o_value[0, p, c] = (adj * key_in[0, p, c].astype(F32)).astype(BF)
        for i, (src, dst) in enumerate(
            ((o_query, out_query), (o_key, out_key), (o_value, out_value))
        ):
            store = pltpu.make_async_copy(src.at[:, :, c], dst.at[:, :, c], store_sem.at[2 * i + h])
            store.start()
            stores.append(store)

    stores = []
    loads[0].wait()
    loads[1].wait()
    loads[2].wait()
    loads[3].wait()
    transpose_gd(0)
    pack_gd(0)
    pl.semaphore_wait(barrier, SEQ + DP - 2)
    exchange(0, s_gd, r_gd, 0)
    pack_gd(1)
    exchange(1, s_gd, r_gd, 512)
    loads[4].wait()
    pack_taps(0)
    exchange(4, s_taps, r_taps, 0)
    transpose_gd(1)
    pack_gd(2)
    exchange(2, s_gd, r_gd, 1024)
    pack_gd(3)
    loads[5].wait()
    loads[6].wait()
    arrived(0, r_gd, 0)
    gate_chunk(0)
    arrived(1, r_gd, 512)
    gate_chunk(1)
    sum_chunk(0)
    exchange(3, s_gd, r_gd, 1536)
    pack_taps(1)
    exchange(5, s_taps, r_taps, 512)
    arrived(4, r_taps, 0)
    forward_taps(0)
    forward_taps(1)
    return_chunk(0)
    send_chunk(0)
    arrived(2, r_gd, 1024)
    gate_chunk(2)
    sum_chunk(1)
    spread_chunk(0)
    return_chunk(1)
    send_chunk(1)
    arrived(3, r_gd, 1536)
    gate_chunk(3)
    sum_chunk(2)
    arrived(5, r_taps, 512)
    forward_taps(2)
    return_chunk(2)
    spread_chunk(1)
    forward_taps(3)
    sum_chunk(3)
    send_chunk(2)
    return_chunk(3)
    send_chunk(3)
    unpack_chunk(0)
    unpack_chunk(1)
    finish(0)
    spread_chunk(2)
    unpack_filter(0)
    spread_chunk(3)
    unpack_filter(1)
    finish_filter(0)
    unpack_chunk(2)
    unpack_chunk(3)
    finish(1)
    unpack_filter(2)
    unpack_filter(3)
    finish_filter(1)

    for index in range(10):
        part = s_gd.at[pl.ds(0, 496)]
        pltpu.make_async_copy(part, part, x_send.at[index]).wait()
    for p in range(4):
        part = z_sum.at[0, pl.ds(0, SEQ - 1)]
        pltpu.make_async_copy(part, part, m_send.at[p]).wait()
        part = z_part.at[pl.ds(0, 192)]
        pltpu.make_async_copy(part, part, rs_send.at[p]).wait()
        part = z_all.at[pl.ds(0, DP - 1), 0]
        pltpu.make_async_copy(part, part, ag_send.at[p]).wait()
    for store in stores:
        store.wait()


def store_kernel(*refs):
    ins, outs, held = refs[:4], refs[4:8], refs[8:12]
    loads = [pltpu.make_async_copy(ins[i], held[i], refs[12].at[i]) for i in range(4)]
    stores = [pltpu.make_async_copy(held[i], outs[i], refs[13].at[i]) for i in range(4)]
    for load in loads:
        load.start()
    for load, store in zip(loads, stores):
        load.wait()
        store.start()
    for store in stores:
        store.wait()


def shards(query, key_in, value, grad_out, filter_taps):
    tables = tuple(jnp.asarray(t) for t in make_tables())
    operands = (query, key_in, value, grad_out, filter_taps, *tables)
    results = (
        jax.ShapeDtypeStruct(query.shape, BF),
        jax.ShapeDtypeStruct(query.shape, BF),
        jax.ShapeDtypeStruct(query.shape, BF),
        jax.ShapeDtypeStruct(filter_taps.shape, F32),
    )

    def block(rows, lanes=LANES):
        return pltpu.VMEM((rows, lanes), F32)

    outs = pl.pallas_call(
        kernel,
        out_shape=results,
        in_specs=[pl.BlockSpec(memory_space=pl.ANY)] * 7,
        out_specs=(pl.BlockSpec(memory_space=pl.ANY),) * 4,
        scratch_shapes=[pltpu.VMEM(x.shape, x.dtype) for x in operands + results]
        + [block(2048), block(1024), block(1024), block(2048), block(1024)]
        + [block(2048), block(2048), block(1024), block(1024), block(2048), block(2048)]
        + [block(2048, 2 * LANES), block(1024, 2 * LANES), block(1024), block(768)]
        + [pltpu.VMEM((4, SEQ, 2, LANES), F32), pltpu.VMEM((DP, 4, SEQ, 2, LANES), F32)]
        + [pltpu.SemaphoreType.DMA((n,)) for n in (10, 10, 4, 4, 4, 4, 4, 4)]
        + [pltpu.SemaphoreType.DMA((7,)), pltpu.SemaphoreType.DMA((8,))],
        compiler_params=pltpu.CompilerParams(
            collective_id=0, has_side_effects=True, vmem_limit_bytes=61 * 1024 * 1024
        ),
    )(*operands)
    return pl.pallas_call(
        store_kernel,
        out_shape=results,
        in_specs=[pl.BlockSpec(memory_space=pl.ANY)] * 4,
        out_specs=(pl.BlockSpec(memory_space=pl.ANY),) * 4,
        scratch_shapes=[pltpu.VMEM(x.shape, x.dtype) for x in results]
        + [pltpu.SemaphoreType.DMA((4,))] * 2,
        compiler_params=pltpu.CompilerParams(
            has_side_effects=True, vmem_limit_bytes=61 * 1024 * 1024
        ),
    )(*outs)


def solution(mesh):
    wide = P("dp", "seq", "tp")
    narrow = P("seq", "tp")
    return jax.shard_map(
        shards,
        mesh=mesh,
        in_specs=(wide, wide, wide, wide, narrow),
        out_specs=(wide, wide, wide, narrow),
        check_vma=False,
    )
```

```python
import functools
import math

import jax
import jax.numpy as jnp
import ml_dtypes
import numpy as np
from jax import lax
from jax.experimental import pallas as pl
from jax.experimental.pallas import tpu as pltpu
from jax.sharding import PartitionSpec as P

MESH = pl.DeviceIdType.MESH
SEQ = 32
DP = 4
LANES = 128
ROWS = 1024
POINTS = 16384
BF = jnp.bfloat16
F32 = jnp.float32


def halves(table):
    table = np.asarray(table, np.float32)
    high = table.astype(ml_dtypes.bfloat16)
    low = (table - high.astype(np.float32)).astype(ml_dtypes.bfloat16)
    return high, low


def make_tables():
    idx = np.arange(LANES, dtype=np.float64)
    turn = 2.0 * math.pi * np.outer(idx + 0.25, idx) / LANES
    first = np.concatenate([np.cos(turn), -np.sin(turn)], axis=0)
    twist = 2.0 * math.pi * np.outer(idx + 0.25, idx) / POINTS
    plain = 2.0 * math.pi * np.outer(idx, idx) / LANES
    cos, sin = np.cos(plain), np.sin(plain)
    second = np.block([[cos, -sin], [sin, cos]])
    back = np.block([[cos, sin], [-sin, cos]])
    last = np.concatenate([np.cos(turn).T, -np.sin(turn).T], axis=1) / POINTS
    first_h, first_l = halves(first)
    mats = [
        np.concatenate([first_h, first_h], axis=1),
        np.concatenate([first_l, np.zeros_like(first_l)], axis=1),
        *halves(second),
        *halves(back),
        *halves(last),
    ]
    turns = [np.cos(twist), -np.sin(twist)]
    return np.concatenate(mats, axis=0), np.concatenate(turns, axis=0).astype(np.float32)


def split(x):
    high = x.astype(BF)
    return high, (x - high.astype(F32)).astype(BF)


def dot(a, b):
    return jnp.dot(a, b, preferred_element_type=F32)


def kernel(
    query_in, key_hbm, value_in, grad_in, taps_in, mats_in, turns_in,
    out_query, out_key, out_value, out_filter,
    query, key_in, value, grad, taps, mats, turns,
    o_query, o_key, o_value, o_filter,
    t_gd, t_taps, t_corr, t_ret, t_filt,
    s_gd, r_gd, s_taps, r_taps, s_ret, r_ret,
    f_gd, f_taps, c_part, z_part, z_sum, z_all,
    x_send, x_recv, m_send, m_recv, rs_send, rs_recv, ag_send, ag_recv,
    load_sem, store_sem,
):
    dp = lax.axis_index("dp")
    me = lax.axis_index("seq")
    tp = lax.axis_index("tp")
    chip, core = me // 2, lax.rem(me, 2)
    x_at, y_at = chip // 4, lax.rem(chip, 4)

    moves = [
        (src.at[:, :, pl.ds(LANES * h, LANES)], dst.at[:, :, pl.ds(LANES * h, LANES)])
        for h in range(2)
        for src, dst in ((key_hbm, key_in), (value_in, value), (grad_in, grad), (query_in, query))
    ] + [(taps_in, taps), (mats_in, mats), (turns_in, turns)]
    loads = [
        pltpu.make_async_copy(src, dst, load_sem.at[i]) for i, (src, dst) in enumerate(moves)
    ]
    for load in loads[:4]:
        load.start()
    first_cat = mats.at[pl.ds(0, 256)]
    first_l = mats.at[pl.ds(256, 256), pl.ds(0, LANES)]
    second_h, second_l, back_h, back_l = (mats.at[pl.ds(512 + 256 * i, 256)] for i in range(4))
    last_h, last_l = (mats.at[pl.ds(1536 + LANES * i, LANES)] for i in range(2))
    turn_re, turn_im = (turns.at[pl.ds(LANES * i, LANES)] for i in range(2))

    at_x = [lax.rem(x_at + d, 4) * 8 for d in (2, 3, 1, 0)]
    at_y = [lax.rem(y_at + d, 4) * 2 for d in (2, 3, 1, 0)]
    at_core = [1 - core, core]
    partners = [x + y + c for c in at_core for x in at_x for y in at_y][:-1]

    barrier = pltpu.get_barrier_semaphore()

    for to in partners:
        pl.semaphore_signal(barrier, inc=1, device_id=(dp, to, tp), device_id_type=MESH)

    for step in range(1, DP):
        pl.semaphore_signal(
            barrier, inc=1, device_id=(lax.rem(dp + step, DP), me, tp), device_id_type=MESH
        )


    def exchange(index, src, dst, base):
        mine = pl.ds(pl.multiple_of(base + me * 16, 16), 16)

        for to in partners:
            pltpu.make_async_remote_copy(
                src_ref=src.at[pl.ds(pl.multiple_of(base + to * 16, 16), 16)],
                dst_ref=dst.at[mine],
                send_sem=x_send.at[index],
                recv_sem=x_recv.at[index],
                device_id=(dp, to, tp),
                device_id_type=MESH,
            ).start()

        pltpu.make_async_copy(src.at[mine], dst.at[mine], x_recv.at[index]).start()

    def arrived(index, dst, base):
        part = dst.at[pl.ds(base, 512)]
        pltpu.make_async_copy(part, part, x_recv.at[index]).wait()


    def transpose_gd(h):
        c = pl.ds(LANES * h, LANES)
        for sig, (left, right) in enumerate(((key_in, value), (grad, query))):
            for a in range(4):
                p = pl.ds(LANES * a, LANES)
                at = ((h * 2 + sig) * 4 + a) * LANES
                t_gd[pl.ds(at, LANES), :] = (left[0, p, c].astype(F32) * right[0, p, c].astype(F32)).T

    def pack_gd(p):
        for sig in range(2):
            for a in range(4):
                at = (((p // 2) * 2 + sig) * 4 + a) * LANES + 64 * (p % 2)
                for c in range(2):
                    s_gd[pl.ds(p * 512 + a * 4 + sig * 2 + c, 32, stride=16), :] = t_gd[
                        pl.ds(at + c, 32, stride=2), :
                    ]

    def pack_taps(h):
        for a in range(4):
            at = (h * 4 + a) * LANES
            t_taps[pl.ds(at, LANES), :] = taps[pl.ds(LANES * a, LANES), pl.ds(LANES * h, LANES)].T
            for v in range(4):
                s_taps[pl.ds(h * 512 + a * 4 + v, 32, stride=16), :] = t_taps[
                    pl.ds(at + 64 * (v // 2) + v % 2, 32, stride=2), :
                ]


    def forward(src, base):
        y = jnp.concatenate([src[pl.ds(base + j, LANES, stride=4), :] for j in range(2)], axis=1)
        yh, yl = split(y)
        a = dot(first_cat[...], jnp.concatenate([yh, yl], axis=0)) + dot(first_l[...], yh)
        wr, wi = turn_re[...], turn_im[...]
        rows = []
        for j in range(2):
            re, im = a[:LANES, LANES * j : LANES * (j + 1)], a[LANES:, LANES * j : LANES * (j + 1)]
            rows.append(jnp.concatenate([re * wr - im * wi, re * wi + im * wr], axis=1))
        ph, pw = split(jnp.concatenate(rows, axis=0))
        return dot(ph, second_h[...]) + dot(pw, second_h[...]) + dot(ph, second_l[...])

    def inverse(left, right, conj):
        lr, li, rr, ri = left[:, :LANES], left[:, LANES:], right[:, :LANES], right[:, LANES:]
        if conj:
            prod = [lr * rr + li * ri, lr * ri - li * rr]
        else:
            prod = [lr * rr - li * ri, lr * ri + li * rr]
        ph, pw = split(jnp.concatenate(prod, axis=1))
        b = dot(ph, back_h[...]) + dot(pw, back_h[...]) + dot(ph, back_l[...])
        wr, wi = turn_re[...], turn_im[...]
        cols = []
        for j in range(2):
            re, im = b[LANES * j : LANES * (j + 1), :LANES], b[LANES * j : LANES * (j + 1), LANES:]
            cols.append(jnp.concatenate([re * wr + im * wi, im * wr - re * wi], axis=0))
        zh, zl = split(jnp.concatenate(cols, axis=1))
        return dot(last_h[...], zh) + dot(last_h[...], zl) + dot(last_l[...], zh)

    def spec_at(p, sig):
        return pl.ds((p * 2 + sig) * 256, 256)

    def gate_chunk(p):
        gate = forward(r_gd, p * 512)
        dgate = forward(r_gd, p * 512 + 2)
        f_gd[spec_at(p, 0), :] = gate
        f_gd[spec_at(p, 1), :] = dgate
        y = inverse(gate, dgate, True)
        for c in range(2):
            at = (p * 2 + c) * LANES
            t_corr[pl.ds(at, LANES), :] = y[:, LANES * c : LANES * (c + 1)]
            for a in range(4):
                c_part[pl.ds(p * 256 + a * 64 + c, 32, stride=2), :] = t_corr[
                    pl.ds(at + a, 32, stride=4), :
                ]
        for step in range(1, DP):
            to = lax.rem(dp + step, DP)
            pltpu.make_async_remote_copy(
                src_ref=c_part.at[pl.ds(pl.multiple_of(p * 256 + to * 64, 64), 64)],
                dst_ref=z_part.at[pl.ds((p * 3 + step - 1) * 64, 64)],
                send_sem=rs_send.at[p],
                recv_sem=rs_recv.at[p],
                device_id=(to, me, tp),
                device_id_type=MESH,
            ).start()

    def sum_chunk(p):
        part = z_part.at[pl.ds(p * 192, 192)]
        pltpu.make_async_copy(part, part, rs_recv.at[p]).wait()
        scale = 1.0 / math.sqrt(DP * POINTS)
        for c in range(2):
            total = c_part[pl.ds(p * 256 + dp * 64 + c, 32, stride=2), :]
            for step in range(DP - 1):
                total = total + z_part[pl.ds((p * 3 + step) * 64 + c, 32, stride=2), :]
            z_sum[:, 2 * p + c, :] = total * scale
        two = pl.ds(2 * p, 2)

        for to in partners:
            pltpu.make_async_remote_copy(
                src_ref=z_sum.at[to, two],
                dst_ref=z_all.at[dp, me, two],
                send_sem=m_send.at[p],
                recv_sem=m_recv.at[p],
                device_id=(dp, to, tp),
                device_id_type=MESH,
            ).start()

        pltpu.make_async_copy(z_sum.at[me, two], z_all.at[dp, me, two], m_recv.at[p]).start()

    def spread_chunk(p):
        part = z_all.at[dp, :, pl.ds(2 * p, 2)]
        pltpu.make_async_copy(part, part, m_recv.at[p]).wait()
        for step in range(1, DP):
            pltpu.make_async_remote_copy(
                src_ref=part,
                dst_ref=part,
                send_sem=ag_send.at[p],
                recv_sem=ag_recv.at[p],
                device_id=(lax.rem(dp + step, DP), me, tp),
                device_id_type=MESH,
            ).start()

    def forward_taps(p):
        f_taps[pl.ds(p * 256, 256), :] = forward(r_taps, (p // 2) * 512 + 2 * (p % 2))

    def return_chunk(p):
        filt = f_taps[pl.ds(p * 256, 256), :]
        conv = inverse(filt, f_gd[spec_at(p, 0), :], False)
        adj = inverse(filt, f_gd[spec_at(p, 1), :], True)
        for v in range(4):
            y = (conv, adj)[v // 2]
            s_ret[pl.ds(p * 512 + v, LANES, stride=4), :] = y[:, LANES * (v % 2) : LANES * (v % 2 + 1)]

    def send_chunk(p):
        exchange(6 + p, s_ret, r_ret, p * 512)

    def unpack_chunk(p):
        arrived(6 + p, r_ret, p * 512)
        for sig in range(2):
            for a in range(4):
                at = (((p // 2) * 2 + sig) * 4 + a) * LANES + 64 * (p % 2)
                for c in range(2):
                    t_ret[pl.ds(at + c, 32, stride=2), :] = r_ret[
                        pl.ds(p * 512 + a * 4 + sig * 2 + c, 32, stride=16), :
                    ]

    def unpack_filter(p):
        part = z_all.at[pl.ds(0, DP - 1), :, pl.ds(2 * p, 2)]
        pltpu.make_async_copy(part, part, ag_recv.at[p]).wait()
        for a in range(4):
            at = ((p // 2) * 4 + a) * LANES + 64 * (p % 2)
            for c in range(2):
                t_filt[pl.ds(at + c, 32, stride=2), :] = z_all[a, :, 2 * p + c, :]

    def finish_filter(h):
        c = pl.ds(LANES * h, LANES)
        for a in range(4):
            o_filter[pl.ds(LANES * a, LANES), c] = t_filt[pl.ds((h * 4 + a) * LANES, LANES), :].T
        store(o_filter.at[:, c], out_filter.at[:, c])

    def store(src, dst):
        copy = pltpu.make_async_copy(src, dst, store_sem.at[len(stores)])
        copy.start()
        stores.append(copy)

    def finish(h):
        c = pl.ds(LANES * h, LANES)
        for a in range(4):
            p = pl.ds(LANES * a, LANES)
            conv = t_ret[pl.ds(((h * 2 + 0) * 4 + a) * LANES, LANES), :].T
            adj = t_ret[pl.ds(((h * 2 + 1) * 4 + a) * LANES, LANES), :].T
            o_query[0, p, c] = (grad[0, p, c].astype(F32) * conv).astype(BF)
            o_key[0, p, c] = (adj * value[0, p, c].astype(F32)).astype(BF)
            o_value[0, p, c] = (adj * key_in[0, p, c].astype(F32)).astype(BF)
            if a % 2 == 1:
                two = pl.ds(LANES * (a - 1), 2 * LANES)
                store(o_query.at[:, two, c], out_query.at[:, two, c])
                store(o_key.at[:, two, c], out_key.at[:, two, c])
                store(o_value.at[:, two, c], out_value.at[:, two, c])

    stores = []
    for load in loads[:4]:
        load.wait()
    for load in loads[4:]:
        load.start()
    transpose_gd(0)
    pack_gd(0)
    pl.semaphore_wait(barrier, SEQ + DP - 2)
    exchange(0, s_gd, r_gd, 0)
    pack_gd(1)
    exchange(1, s_gd, r_gd, 512)
    loads[8].wait()
    pack_taps(0)
    exchange(4, s_taps, r_taps, 0)
    for load in loads[4:8]:
        load.wait()
    transpose_gd(1)
    pack_gd(2)
    exchange(2, s_gd, r_gd, 1024)
    pack_gd(3)
    loads[9].wait()
    loads[10].wait()
    arrived(0, r_gd, 0)
    gate_chunk(0)
    arrived(1, r_gd, 512)
    gate_chunk(1)
    sum_chunk(0)
    exchange(3, s_gd, r_gd, 1536)
    pack_taps(1)
    exchange(5, s_taps, r_taps, 512)
    arrived(4, r_taps, 0)
    forward_taps(0)
    forward_taps(1)
    return_chunk(0)
    send_chunk(0)
    arrived(2, r_gd, 1024)
    gate_chunk(2)
    sum_chunk(1)
    spread_chunk(0)
    return_chunk(1)
    send_chunk(1)
    arrived(3, r_gd, 1536)
    gate_chunk(3)
    sum_chunk(2)
    arrived(5, r_taps, 512)
    forward_taps(2)
    return_chunk(2)
    spread_chunk(1)
    forward_taps(3)
    sum_chunk(3)
    send_chunk(2)
    return_chunk(3)
    send_chunk(3)
    unpack_chunk(0)
    unpack_chunk(1)
    finish(0)
    spread_chunk(2)
    unpack_filter(0)
    spread_chunk(3)
    unpack_filter(1)
    finish_filter(0)
    unpack_chunk(2)
    unpack_chunk(3)
    finish(1)
    unpack_filter(2)
    unpack_filter(3)
    finish_filter(1)

    for index in range(10):
        part = s_gd.at[pl.ds(0, 496)]
        pltpu.make_async_copy(part, part, x_send.at[index]).wait()
    for p in range(4):
        part = z_sum.at[pl.ds(0, SEQ - 1), pl.ds(0, 2)]
        pltpu.make_async_copy(part, part, m_send.at[p]).wait()
        part = z_part.at[pl.ds(0, 192)]
        pltpu.make_async_copy(part, part, rs_send.at[p]).wait()
        part = z_all.at[pl.ds(0, DP - 1), :, pl.ds(0, 2)]
        pltpu.make_async_copy(part, part, ag_send.at[p]).wait()
    for copy in stores:
        copy.wait()


def store_kernel(*refs):
    ins, outs, held = refs[:4], refs[4:8], refs[8:12]
    loads = [pltpu.make_async_copy(ins[i], held[i], refs[12].at[i]) for i in range(4)]
    stores = [pltpu.make_async_copy(held[i], outs[i], refs[13].at[i]) for i in range(4)]
    for load in loads:
        load.start()
    for load, store in zip(loads, stores):
        load.wait()
        store.start()
    for store in stores:
        store.wait()


def shards(query, key_in, value, grad_out, filter_taps):
    tables = tuple(jnp.asarray(t) for t in make_tables())
    operands = (query, key_in, value, grad_out, filter_taps, *tables)
    results = (
        jax.ShapeDtypeStruct(query.shape, BF),
        jax.ShapeDtypeStruct(query.shape, BF),
        jax.ShapeDtypeStruct(query.shape, BF),
        jax.ShapeDtypeStruct(filter_taps.shape, F32),
    )

    def block(rows, lanes=LANES):
        return pltpu.VMEM((rows, lanes), F32)

    outs = pl.pallas_call(
        kernel,
        out_shape=results,
        in_specs=[pl.BlockSpec(memory_space=pl.ANY)] * 7,
        out_specs=(pl.BlockSpec(memory_space=pl.ANY),) * 4,
        scratch_shapes=[pltpu.VMEM(x.shape, x.dtype) for x in operands + results]
        + [block(2048), block(1024), block(1024), block(2048), block(1024)]
        + [block(2048), block(2048), block(1024), block(1024), block(2048), block(2048)]
        + [block(2048, 2 * LANES), block(1024, 2 * LANES), block(1024), block(768)]
        + [pltpu.VMEM((SEQ, 8, LANES), F32), pltpu.VMEM((DP, SEQ, 8, LANES), F32)]
        + [pltpu.SemaphoreType.DMA((n,)) for n in (10, 10, 4, 4, 4, 4, 4, 4)]
        + [pltpu.SemaphoreType.DMA((11,)), pltpu.SemaphoreType.DMA((14,))],
        compiler_params=pltpu.CompilerParams(
            collective_id=0, has_side_effects=True, vmem_limit_bytes=61 * 1024 * 1024
        ),
    )(*operands)
    return pl.pallas_call(
        store_kernel,
        out_shape=results,
        in_specs=[pl.BlockSpec(memory_space=pl.ANY)] * 4,
        out_specs=(pl.BlockSpec(memory_space=pl.ANY),) * 4,
        scratch_shapes=[pltpu.VMEM(x.shape, x.dtype) for x in results]
        + [pltpu.SemaphoreType.DMA((4,))] * 2,
        compiler_params=pltpu.CompilerParams(
            has_side_effects=True, vmem_limit_bytes=61 * 1024 * 1024
        ),
    )(*outs)


def solution(mesh):
    wide = P("dp", "seq", "tp")
    narrow = P("seq", "tp")
    return jax.shard_map(
        shards,
        mesh=mesh,
        in_specs=(wide, wide, wide, wide, narrow),
        out_specs=(wide, wide, wide, narrow),
        check_vma=False,
    )
```
